32 devices in a mesh: replica: 8 (over y, x, core), shard: 4 (over z).
Axes of the slice: x: 2, y: 2, z: 4, core: 2. Of those that a mesh axis runs over, the one named last changes fastest.
Arguments:
- inputs: bfloat16 [8, 1024, 1024], P('replica', 'shard'), may hold values from -6 to 6
- out_grad: bfloat16 [8, 1024, 1024], P('replica', 'shard'), may hold values from -6 to 6
- segment_ids: int32 [8, 1024], P('replica'), may hold values from 0 to 2, never falling along the last dimension, each value on 1 to 512 neighbouring positions
- ln_gain_attn: bfloat16 [1024], P('shard'), may hold values from 0.5 to 1.5
- ln_bias_attn: bfloat16 [1024], P('shard'), may hold values from -3 to 3
- ln_gain_mlp: bfloat16 [1024], P('shard'), may hold values from 0.5 to 1.5
- ln_bias_mlp: bfloat16 [1024], P('shard'), may hold values from -3 to 3
- qkv_weight: bfloat16 [1024, 3072], P('shard'), may hold values from -0.1875 to 0.1875
- qkv_bias: bfloat16 [3072], P('shard'), may hold values from -3 to 3
- out_weight: bfloat16 [1024, 1024], P('shard'), may hold values from -0.75 to 0.75
- up_weight: bfloat16 [1024, 4096], P('shard'), may hold values from -0.1875 to 0.1875
- up_bias: bfloat16 [4096], P('shard'), may hold values from -3 to 3
- down_weight: bfloat16 [4096, 1024], P('shard'), may hold values from -0.09375 to 0.09375
- output_bias: bfloat16 [1024], P('shard'), may hold values from -3 to 3
Outputs:
- outputs: bfloat16 [8, 1024, 1024], P('replica', 'shard')
- in_grad: bfloat16 [8, 1024, 1024], P('replica', 'shard')
- grad_ln_gain_attn: float32 [1024], P('shard')
- grad_ln_bias_attn: float32 [1024], P('shard')
- grad_ln_gain_mlp: float32 [1024], P('shard')
- grad_ln_bias_mlp: float32 [1024], P('shard')
- grad_qkv_weight: float32 [1024, 3072], P('shard')
- grad_qkv_bias: float32 [3072], P('shard')
- grad_out_weight: float32 [1024, 1024], P('shard')
- grad_up_weight: float32 [1024, 4096], P('shard')
- grad_up_bias: float32 [4096], P('shard')
- grad_down_weight: float32 [4096, 1024], P('shard')
- grad_output_bias: float32 [1024], P('shard')
The draws below stay inside these ranges and needn't reach their ends.
Inputs may be any that keep to these rules, and one draw needn't show every extreme that they name: `segment_ids`: in every sequence the document numbers never fall and run through 0 to 2; every document has 1 to 512 tokens, one exactly 512.
All inputs are finite; a program needn't handle non-finite values.
Results may differ from the reference program's by a relative error of at most 0.012.
Values may be sent and summed in bfloat16 or wider, within the bound.
A program may use at most 256 MiB of HBM per device.

```python
import math
from functools import partial
import jax
import jax.numpy as jnp
import numpy as np
from jax import lax

D = 1024
FF = 4096
HEADS = 16
HEAD = 64
ROT = 16
SEQ_LEN = 1024
DOCS = 3
BATCH = 8


def shard_levels(own_key, extent, pieces, smallest, largest):
    factor_of, own = 1.0, jax.random.fold_in(own_key, 6)
    for axis_at, parts in pieces:
        steps = jnp.exp(jax.random.uniform(jax.random.fold_in(own, axis_at), (parts,), jnp.float32, smallest / len(pieces), largest / len(pieces)))
        factor_of = factor_of * jnp.repeat(steps, extent[axis_at] // parts).reshape([-1 if axis == axis_at else 1 for axis in range(len(extent))])
    return factor_of


def length_profile(number_of, total, reach, skew):
    portions = [(1 << 20) // math.isqrt(standing ** skew) + 1 for standing in range(2, number_of + 1)]
    rest, given = total - reach - (number_of - 1), [1] * (number_of - 1)
    while rest > 0:
        movable = [i for i in range(number_of - 1) if given[i] < reach]
        pool, left = sum([portions[i] for i in movable]), rest
        for i in movable:
            addition = min(reach - given[i], max(1, left * portions[i] // pool), rest)
            given[i] = given[i] + addition
            rest = rest - addition
    return np.array([reach] + given)


def uneven(own_key, number_of, total, bound, slope):
    if number_of == 2:
        one = jax.random.randint(own_key, (), max(1, total - bound), min(bound, total - 1) + 1)
        return jnp.stack([one, total - one])
    sizes = jnp.asarray(length_profile(number_of, total, bound, slope), jnp.int32)
    couples = (number_of - 1) // 2
    donor, taker = sizes[1:1 + 2 * couples:2], sizes[2:2 + 2 * couples:2]
    slack = jnp.minimum(donor - 1, bound - taker)
    shifted = jax.random.randint(jax.random.fold_in(own_key, 1), (couples,), 0, 1 << 20) % (slack + 1)
    sizes = sizes.at[1:1 + 2 * couples:2].set(donor - shifted).at[2:2 + 2 * couples:2].set(taker + shifted)
    return sizes[jax.random.permutation(jax.random.fold_in(own_key, 2), number_of)]


def centred(rng, extent, spread, bound, cuts=(), kind=jnp.bfloat16):
    entries = jax.random.normal(rng, extent, jnp.float32) * spread
    if len(cuts) > 0:
        entries = shard_levels(rng, extent, cuts, -0.22, 0.18) * entries
    return jnp.clip(entries, min=-bound, max=bound).astype(kind)


def setup_inputs(seed: int = 0) -> dict:
    key_list = jax.random.split(jax.random.key(seed), 15)
    return {
        "inputs": centred(key_list[0], (BATCH, SEQ_LEN, D), 1.0, 6.0, ((0, 8), (1, 4))),
        "out_grad": centred(key_list[1], (BATCH, SEQ_LEN, D), 1.0, 6.0, ((0, 8), (1, 4))),
        "segment_ids": jax.vmap(lambda own: jnp.searchsorted(jnp.cumsum(uneven(own, DOCS, SEQ_LEN, SEQ_LEN // 2, 0)), jnp.arange(SEQ_LEN), side="right"))(jax.random.split(key_list[2], BATCH)).reshape((BATCH, SEQ_LEN)).astype(jnp.int32),
        "ln_gain_attn": jnp.clip(1.0 + 0.1 * jax.random.normal(key_list[3], (D,), jnp.float32), 0.5, 1.5).astype(jnp.bfloat16),
        "ln_bias_attn": centred(key_list[4], (D,), 0.5, 3.0, ((0, 4),)),
        "ln_gain_mlp": jnp.clip(1.0 + 0.1 * jax.random.normal(key_list[5], (D,), jnp.float32), 0.5, 1.5).astype(jnp.bfloat16),
        "ln_bias_mlp": centred(key_list[6], (D,), 0.5, 3.0, ((0, 4),)),
        "qkv_weight": centred(key_list[7], (D, 3 * D), D ** -0.5, 0.1875, ((0, 4),)),
        "qkv_bias": centred(key_list[8], (3 * D,), 0.5, 3.0, ((0, 4),)),
        "out_weight": centred(key_list[9], (D, D), (D // 16) ** -0.5, 0.75, ((0, 4),)),
        "up_weight": centred(key_list[10], (D, FF), D ** -0.5, 0.1875, ((0, 4),)),
        "up_bias": centred(key_list[11], (FF,), 0.5, 3.0, ((0, 4),)),
        "down_weight": centred(key_list[12], (FF, D), FF ** -0.5, 0.09375, ((0, 4),)),
        "output_bias": centred(key_list[13], (D,), 0.5, 3.0, ((0, 4),)),
    }


@jax.custom_vjp
def low(v):
    return lax.optimization_barrier(v.astype(jnp.bfloat16)).astype(jnp.float32)

@jax.custom_vjp
def low_back(v):
    return v

def low_keep(v):
    return (low(v), None)

def low_pass(kept, grad):
    return (grad,)

def back_keep(v):
    return (v, None)

def back_low(kept, grad):
    return (low(grad),)
low.defvjp(low_keep, low_pass)
low_back.defvjp(back_keep, back_low)

def matmul(left, right):
    return jnp.dot(left, right, precision=lax.Precision.HIGHEST, preferred_element_type=jnp.float32)

def layer_norm(values, gain, shift):
    centered = values - lax.optimization_barrier(jnp.mean(values, axis=-1, keepdims=True))
    variance = lax.optimization_barrier(jnp.mean(centered * centered, axis=-1, keepdims=True))
    return centered * lax.rsqrt(variance + 1e-05) * gain + shift

def doc_positions(segment_row):
    documents = jnp.arange(DOCS, dtype=jnp.int32)
    member = (segment_row[:, None] == documents[None, :]).astype(jnp.int32)
    counts = lax.optimization_barrier(jnp.sum(member, axis=0)).astype(jnp.int32)
    starts = (jnp.cumsum(counts) - counts).astype(jnp.int32)
    doc_start = lax.optimization_barrier(jnp.sum(member * starts[None, :], axis=1)).astype(jnp.int32)
    return jnp.arange(segment_row.shape[0], dtype=jnp.int32) - doc_start

def rotate(features, positions):
    half_rot = ROT // 2
    inv_freq = 1.0 / 10000.0 ** (jnp.arange(half_rot, dtype=jnp.float32) * 2.0 / ROT)
    angles = positions.astype(jnp.float32)[..., None] * inv_freq
    cosine = jnp.cos(angles)[..., None, :]
    sine_part = jnp.sin(angles)[..., None, :]
    front_half = features[..., :half_rot]
    back_half = features[..., half_rot:ROT]
    return jnp.concatenate([front_half * cosine - back_half * sine_part, back_half * cosine + front_half * sine_part, features[..., ROT:]], axis=-1)

def attend(element):
    queries, key_rows, value_rows, segment_row = element
    length = segment_row.shape[0]
    position = jnp.arange(length, dtype=jnp.int32)
    allowed = (position[None, :] <= position[:, None]) & (segment_row[None, :] == segment_row[:, None])
    scores = jnp.einsum('qhd,khd->hqk', queries, key_rows, precision=lax.Precision.HIGHEST) * HEAD ** (-0.5)
    scores = low_back(jnp.where(allowed[None], scores, -1e+30))
    weights = low(jax.nn.softmax(scores, axis=-1))
    return jnp.einsum('hqk,khd->qhd', weights, value_rows, precision=lax.Precision.HIGHEST)

def forward(segment_ids, inputs, ln_gain_attn, ln_bias_attn, ln_gain_mlp, ln_bias_mlp, qkv_weight, qkv_bias, out_weight, up_weight, up_bias, down_weight, output_bias):
    batch_count, length, model_width = inputs.shape
    flat_in = inputs.reshape(batch_count * length, model_width)
    attn_normed = low(layer_norm(flat_in, ln_gain_attn, ln_bias_attn))
    mlp_normed = low(layer_norm(flat_in, ln_gain_mlp, ln_bias_mlp))
    qkv_parts = low_back(matmul(attn_normed, qkv_weight) + qkv_bias).reshape(batch_count, length, 3, HEADS, HEAD)
    positions = jax.vmap(doc_positions)(segment_ids)
    queries = low(rotate(qkv_parts[:, :, 0], positions))
    key_rows = low(rotate(qkv_parts[:, :, 1], positions))
    value_rows = low(qkv_parts[:, :, 2])
    context = lax.map(jax.checkpoint(attend), (queries, key_rows, value_rows, segment_ids))
    context = low(low_back(context.reshape(batch_count * length, model_width)))
    hidden_pre = low_back(matmul(mlp_normed, up_weight) + up_bias)
    hidden = low(jax.nn.gelu(hidden_pre, approximate=False))
    result = flat_in + matmul(context, out_weight) + matmul(hidden, down_weight) + output_bias
    return result.reshape(batch_count, length, model_width)

def reference(inputs, out_grad, segment_ids, ln_gain_attn, ln_bias_attn, ln_gain_mlp, ln_bias_mlp, qkv_weight, qkv_bias, out_weight, up_weight, up_bias, down_weight, output_bias):
    result, pullback = jax.vjp(partial(forward, segment_ids), inputs.astype(jnp.float32), ln_gain_attn.astype(jnp.float32), ln_bias_attn.astype(jnp.float32), ln_gain_mlp.astype(jnp.float32), ln_bias_mlp.astype(jnp.float32), qkv_weight.astype(jnp.float32), qkv_bias.astype(jnp.float32), out_weight.astype(jnp.float32), up_weight.astype(jnp.float32), up_bias.astype(jnp.float32), down_weight.astype(jnp.float32), output_bias.astype(jnp.float32))
    grads = pullback(out_grad.astype(jnp.float32))
    return (result.astype(jnp.bfloat16), grads[0].astype(jnp.bfloat16), grads[1], grads[2], grads[3], grads[4], grads[5], grads[6], grads[7], grads[8], grads[9], grads[10], grads[11])
```

```python
import math
from functools import partial

import jax
import jax.numpy as jnp
from jax import lax
from jax.experimental import pallas as pl
from jax.experimental.pallas import tpu as pltpu
from jax.sharding import PartitionSpec as P

D = 1024
FF = 4096
HEADS = 16
HEAD = 64
ROT = 16
Z = 4
LOC = 256
TOK = 1024
PAIRS = 2
QB = 128
KB = 640
EPS = 1e-05
BF = jnp.bfloat16
F32 = jnp.float32
MESH = pl.DeviceIdType.MESH
NSEM = 256
STAGE = 4


def bit_of(value, place):
    return lax.rem(lax.div(value, 1 << place), 2)


def flip(value, place):
    return value + (1 - 2 * bit_of(value, place)) * (1 << place)


def nn(a, b):
    return jnp.dot(a, b, preferred_element_type=F32)


def nt(a, b):
    return lax.dot_general(a, b, (((1,), (1,)), ((), ())), preferred_element_type=F32)


def tn(a, b):
    return lax.dot_general(a, b, (((0,), (0,)), ((), ())), preferred_element_type=F32)


def blk(i, n):
    return pl.ds(pl.multiple_of(i * n, n), n)


class Count:
    def __init__(self):
        self.used = 0

    def take(self, n):
        first = self.used
        self.used += n
        assert self.used <= NSEM
        return first


def layer(
    replicas,
    stage,
    x_in,
    og_in,
    qkv_w,
    up_w,
    out_w,
    down_w,
    vec_in,
    upb,
    start,
    tab_c,
    tab_a,
    tab_b,
    outputs,
    in_grad,
    f_qkv,
    f_up,
    f_out,
    f_down,
    vec_out,
    x_all,
    og_all,
    vec_all,
    wqkv,
    wup,
    wout,
    wdown,
    attn_n,
    mlp_n,
    mean_s,
    rstd_s,
    q_s,
    k_s,
    v_s,
    ctx,
    lse,
    h32,
    g32,
    acc,
    hidden,
    dgelu,
    part,
    own,
    zrecv,
    zrelay,
    gctx,
    dq,
    dk,
    dv,
    dqkv,
    g_qkv,
    g_up,
    g_out,
    g_down,
    t_qkv,
    t_up,
    t_out,
    t_down,
    vsum,
    vrecv,
    ssem,
    rsem,
    lsem,
):
    r = lax.axis_index("replica")
    z = lax.axis_index("shard")
    bits = int(math.log2(replicas))
    nb = min(bits, 4)
    chunks = 1 << nb
    sends, recvs, locals_ = Count(), Count(), Count()
    pending = []

    def remote(src, dst, s, v, dev):
        return pltpu.make_async_remote_copy(
            src_ref=src,
            dst_ref=dst,
            send_sem=ssem.at[s],
            recv_sem=rsem.at[v],
            device_id=dev,
            device_id_type=MESH,
        )

    def go(src, dst, s, v, dev, when=None):
        copy = remote(src, dst, s, v, dev)
        if when is None:
            copy.start()
        else:
            pl.when(when)(copy.start)
        pending.append((copy, when))

    def arrived(dst, v, when=None):
        copy = remote(dst, dst, 0, v, (r, z))
        if when is None:
            copy.wait_recv()
        else:
            pl.when(when)(copy.wait_recv)

    def local(src, dst):
        copy = pltpu.make_async_copy(src, dst, lsem.at[locals_.take(1)])
        copy.start()
        return copy

    barrier = pltpu.get_barrier_semaphore()
    for step in range(1, Z):
        pl.semaphore_signal(
            barrier, inc=1, device_id=(r, lax.rem(z + step, Z)), device_id_type=MESH
        )
    for b in range(bits):
        pl.semaphore_signal(barrier, inc=1, device_id=(flip(r, b), z), device_id_type=MESH)
    pl.semaphore_wait(barrier, Z - 1 + bits)

    order_a = list(range(nb))
    order_b = [0, *reversed(range(1, nb))]

    def index_of(order):
        return sum(bit_of(r, b) * (1 << (nb - 1 - k)) for k, b in enumerate(order))

    idx_a, idx_b = index_of(order_a), index_of(order_b)
    cr = LOC // chunks

    up_v, qkv_v, vec_v = recvs.take(Z), recvs.take(3 * Z), recvs.take(Z)
    vec_own = local(vec_in, vec_all.at[blk(z, 16)])
    for step in (1, 3, 2):
        t = lax.rem(z + step, Z)
        go(vec_in, vec_all.at[blk(z, 16)], sends.take(1), vec_v + z, (r, t))
        go(
            up_w.at[blk(idx_a, cr), blk(t, 1024)],
            wup.at[pl.ds(pl.multiple_of(z * LOC + idx_a * cr, cr), cr)],
            sends.take(1),
            up_v + z,
            (r, t),
        )
        for s in range(3):
            go(
                qkv_w.at[blk(idx_b, cr), pl.ds(pl.multiple_of(s * D + t * 256, 256), 256)],
                wqkv.at[pl.ds(pl.multiple_of(z * LOC + idx_b * cr, cr), cr), pl.ds(s * 256, 256)],
                sends.take(1),
                qkv_v + z * 3 + s,
                (r, t),
            )
    own_up = local(up_w.at[:, blk(z, 1024)], wup.at[blk(z, LOC)])
    own_qkv = [
        local(
            qkv_w.at[:, pl.ds(pl.multiple_of(s * D + z * 256, 256), 256)],
            wqkv.at[blk(z, LOC), pl.ds(s * 256, 256)],
        )
        for s in range(3)
    ]

    SUB = 2

    class Gather:
        def __init__(self, src, buf):
            self.src, self.buf = src, buf
            self.v = recvs.take(Z * SUB)

        def rows(self, c, k):
            n = LOC // SUB
            return self.buf.at[pl.ds(pl.multiple_of(c * LOC + k * n, n), n)]

        def send(self):
            n = LOC // SUB
            for k in range(SUB):
                for d in (2, -2, 1, -1):
                    t = z + d
                    go(
                        self.src.at[pl.ds(k * n, n)],
                        self.rows(z, k),
                        sends.take(1),
                        self.v + z * SUB + k,
                        (r, jnp.clip(t, 0, Z - 1)),
                        (t >= 0) & (t < Z),
                    )

        def relay(self):
            for k in range(SUB):
                s = sends.take(1)
                for at, frm, to in ((2, 0, 3), (1, 3, 0)):
                    arrived(self.rows(frm, k), self.v + frm * SUB + k, z == at)
                    go(
                        self.rows(frm, k),
                        self.rows(frm, k),
                        s,
                        self.v + frm * SUB + k,
                        (r, to),
                        z == at,
                    )

        def wait(self, c):
            passed = ((z == 2) & (c == 0)) | ((z == 1) & (c == 3))
            for k in range(SUB):
                arrived(self.rows(c, k), self.v + c * SUB + k, jnp.logical_not(passed))

    near = [z, z + 1 - 2 * lax.rem(z, 2), z + 2 - 4 * lax.div(z, 2), 3 - z]
    gx, gg = Gather(x_in, x_all), Gather(og_in, og_all)
    gx.send()
    x_own = local(x_in, x_all.at[blk(z, LOC)])
    og_own = local(og_in, og_all.at[blk(z, LOC)])
    w_own = [local(out_w, wout), local(down_w, wdown)]

    ag_v = recvs.take(3 * 2 * nb)

    def weight_region(kind, zz, first, n):
        ref = wup if kind == 0 else wqkv
        return ref.at[pl.ds(pl.multiple_of(zz * LOC + first * cr, cr), n * cr)]

    def weight_step(k):
        for j in range(1, Z):
            zz = lax.rem(z + j, Z)
            for kind, order, idx in ((0, order_a, idx_a), (1, order_b, idx_b)):
                b = order[nb - 1 - k]
                size = 1 << k
                first = lax.div(idx, size) * size
                go(
                    weight_region(kind, zz, first, size),
                    weight_region(kind, zz, first, size),
                    sends.take(1),
                    ag_v + ((j - 1) * 2 + kind) * nb + k,
                    (flip(r, b), z),
                )

    def weight_wait(k):
        for j in range(1, Z):
            zz = lax.rem(z + j, Z)
            for kind, idx in ((0, idx_a), (1, idx_b)):
                size = 1 << k
                first = flip(lax.div(idx, size), 0) * size
                arrived(weight_region(kind, zz, first, size), ag_v + ((j - 1) * 2 + kind) * nb + k)

    for j in range(1, Z):
        zz = lax.rem(z + j, Z)
        arrived(vec_all.at[blk(zz, 16)], vec_v + zz)
        arrived(weight_region(0, zz, idx_a, 1), up_v + zz)
        for s in range(3):
            arrived(
                wqkv.at[pl.ds(pl.multiple_of(zz * LOC + idx_b * cr, cr), cr), pl.ds(s * 256, 256)],
                qkv_v + zz * 3 + s,
            )
    for k in range(nb):
        weight_step(k)
        if k == nb - 1:
            gx.relay()
        weight_wait(k)
    vec_own.wait()
    x_own.wait()
    og_own.wait()
    own_up.wait()
    for copy in own_qkv + w_own:
        copy.wait()
    for c in near[1:]:
        gx.wait(c)
    gg.send()

    if stage >= 2:
        def vector(row):
            return jnp.concatenate(
                [vec_all[16 * c : 16 * c + 16, :][row : row + 1, :] for c in range(Z)], axis=1
            ).astype(F32)

        def vector256(i):
            block = vec_all[pl.ds(pl.multiple_of(lax.div(i, 3) * 16, 16), 16), :].astype(F32)
            rows = lax.broadcasted_iota(jnp.int32, (16, 256), 0)
            return jnp.sum(jnp.where(rows == 4 + lax.rem(i, 3), block, 0.0), axis=0, keepdims=True)

        gain_a, bias_a, gain_m, bias_m, bias_o = [vector(i) for i in (0, 1, 2, 3, 7)]
        qkv_b = [vector256(s * Z + z) for s in range(3)]

        def norm(i, carry):
            rows = blk(i, 16)
            v = x_all[rows, :].astype(F32)
            mean = jnp.mean(v, axis=1, keepdims=True)
            cen = v - mean
            rstd = lax.rsqrt(jnp.mean(cen * cen, axis=1, keepdims=True) + EPS)
            xhat = cen * rstd
            attn_n[rows, :] = (xhat * gain_a + bias_a).astype(BF)
            mlp_n[rows, :] = (xhat * gain_m + bias_m).astype(BF)
            mean_s[rows, :] = mean
            rstd_s[rows, :] = rstd
            return carry

        lax.fori_loop(0, TOK // 16, norm, 0, unroll=2)

        def rotate(t, rows, sign):
            return (
                t * tab_c[rows, :]
                + sign * (pltpu.roll(t, 120, 1) * tab_a[rows, :])
                + sign * (pltpu.roll(t, 8, 1) * tab_b[rows, :])
            )

        @pl.loop(0, Z)
        def _(c):
            rows = blk(c, LOC)
            res = nn(attn_n[rows, :], wqkv[...])
            for p in range(PAIRS):
                lanes = slice(128 * p, 128 * p + 128)
                t = res[:, lanes] + qkv_b[0][:, lanes]
                q_s[rows, lanes] = (rotate(t, rows, 1.0) * 0.125).astype(BF)
                t = res[:, 256 + 128 * p : 384 + 128 * p] + qkv_b[1][:, lanes]
                k_s[rows, lanes] = rotate(t, rows, 1.0).astype(BF)
            v_s[rows, :] = (res[:, 512:] + qkv_b[2]).astype(BF)

        lane = lax.broadcasted_iota(jnp.int32, (QB, 128), 1)

        def twice(t):
            zero = jnp.zeros_like(t)
            return jnp.concatenate(
                [jnp.where(lane < HEAD, t, zero), jnp.where(lane >= HEAD, t, zero)], axis=0
            )

        def fold(t):
            return jnp.where(lane < HEAD, t[:QB], t[QB:])

        def window(i):
            first = pl.multiple_of(jnp.maximum(i * QB - (KB - QB), 0), QB)
            at = first + lax.broadcasted_iota(jnp.int32, (QB, KB), 1)
            row = i * QB + lax.broadcasted_iota(jnp.int32, (QB, KB), 0)
            ok = (at <= row) & (at >= start[blk(i, QB), :])
            bias = jnp.where(ok, 0.0, -1e30)
            return pl.ds(first, KB), jnp.concatenate([bias, bias], axis=0)

        @pl.loop(0, TOK // QB)
        def _(i):
            keys, bias = window(i)
            rows = blk(i, QB)
            for p in range(PAIRS):
                lanes = slice(128 * p, 128 * p + 128)
                s = nt(twice(q_s[rows, lanes]), k_s[keys, lanes]) + bias
                top = jnp.max(s, axis=1, keepdims=True)
                e = jnp.exp(s - top)
                total = jnp.sum(e, axis=1, keepdims=True)
                lse[p, blk(i, 2 * QB), :] = top + jnp.log(total)
                prob = (e * (1.0 / total)).astype(BF)
                ctx[rows, lanes] = fold(nn(prob, v_s[keys, lanes])).astype(BF)

        up_shift = upb[...]

        @pl.loop(0, Z)
        def _(c):
            h32[...] = nn(mlp_n[blk(c, LOC), :], wup[...])

            def act(i, carry):
                v = h32[blk(i, 16), :] + up_shift
                cdf = 0.5 + 0.5 * lax.erf(v * (0.5**0.5))
                rows = pl.ds(pl.multiple_of(c * LOC + i * 16, 16), 16)
                hidden[rows, :] = (v * cdf).astype(BF)
                dgelu[rows, :] = (
                    cdf + v * jnp.exp(-0.5 * v * v) * (1.0 / math.sqrt(2.0 * math.pi))
                ).astype(BF)
                return carry

            lax.fori_loop(0, LOC // 16, act, 0)

        gg.relay()

        @pl.loop(0, Z)
        def _(j):
            c = lax.rem(z + 1 + j, Z)
            rows = blk(c, LOC)
            res = nn(ctx[rows, :], wout[...]) + nn(hidden[rows, :], wdown[...])

            @pl.when(j < Z - 1)
            def _():
                part[rows, :] = res.astype(BF)

            @pl.when(j == Z - 1)
            def _():
                own[...] = res + x_in[...].astype(F32) + bias_o

    else:
        gg.relay()
    for c in near[1:]:
        gg.wait(c)

    class Scatter:
        def __init__(self, side):
            self.side = side
            self.v = recvs.take(Z)
            self.rv = recvs.take(1)
            self.recv = zrecv.at[pl.ds(side * TOK, TOK)]
            self.hold = zrelay.at[pl.ds(side * LOC, LOC)]

        def send(self):
            s = sends.take(1)
            go(part.at[blk(0, LOC)], self.hold, s, self.rv, (r, 2), z == 3)
            go(part.at[blk(3, LOC)], self.hold, s, self.rv, (r, 1), z == 0)
            for d in (2, -2, 1, -1):
                t = z + d
                ok = (t >= 0) & (t < Z)
                if abs(d) == 2:
                    ok = ok & ((z == 0) | (z == 3))
                self.one(t, ok)

        def one(self, t, ok):
            t = jnp.clip(t, 0, Z - 1)
            go(
                part.at[blk(t, LOC)],
                self.recv.at[blk(z, LOC)],
                sends.take(1),
                self.v + z,
                (r, t),
                ok,
            )

        def relay(self):
            mid = (z == 1) | (z == 2)
            t = jnp.where(z == 1, 3, 0)
            arrived(self.hold, self.rv, mid)

            @pl.when(mid)
            def _():
                def add(i, carry):
                    rows = pl.ds(pl.multiple_of(t * LOC + i * 16, 16), 16)
                    part[rows, :] = part[rows, :] + self.hold[blk(i, 16), :]
                    return carry

                lax.fori_loop(0, LOC // 16, add, 0, unroll=2)

            self.one(t, mid)

        def finish(self):
            for d in (1, -1, 2, -2):
                c = z + d
                ok = (c >= 0) & (c < Z)
                cc = jnp.clip(c, 0, Z - 1)
                arrived(self.recv.at[blk(cc, LOC)], self.v + cc, ok)

                @pl.when(ok)
                def _():
                    def add(i, carry):
                        rows = blk(i, 16)
                        got = self.recv[pl.ds(pl.multiple_of(cc * LOC + i * 16, 16), 16), :]
                        own[rows, :] += got.astype(F32)
                        return carry

                    lax.fori_loop(0, LOC // 16, add, 0, unroll=2)

    def flush():
        for copy, when in [p for p in pending if p is not None]:
            if when is None:
                copy.wait_send()
            else:
                pl.when(when)(copy.wait_send)
        pending.clear()

    if stage >= 3:
        s_out = Scatter(0)
        s_out.send()

        g_out[...] = tn(ctx[...], og_all[...]).astype(BF)

        @pl.loop(0, Z)
        def _(c):
            g_down[blk(c, 256), :] = tn(hidden[:, blk(c, 256)], og_all[...]).astype(BF)

        vsum[...] = jnp.zeros_like(vsum)

        @pl.loop(0, Z)
        def _(c):
            rows = blk(c, LOC)
            gctx[rows, :] = nt(og_all[rows, :], wout[...]).astype(BF)
            h32[...] = nt(og_all[rows, :], wdown[...])

            def act(i, carry):
                at = pl.ds(pl.multiple_of(c * LOC + i * 16, 16), 16)
                g = (h32[blk(i, 16), :] * dgelu[at, :].astype(F32)).astype(BF)
                dgelu[at, :] = g
                return carry + g.astype(F32)

            total = lax.fori_loop(0, LOC // 16, act, jnp.zeros((16, 1024), F32))
            vsum[pl.ds(7 + z, 1), :] += jnp.sum(total, axis=0, keepdims=True)

        dhid = dgelu
        s_out.relay()

        acc[...] = jnp.zeros_like(acc)
        dk[...] = jnp.zeros_like(dk)
        dv[...] = jnp.zeros_like(dv)

        @pl.loop(0, TOK // QB)
        def _(i):
            keys, bias = window(i)
            rows = blk(i, QB)
            for p in range(PAIRS):
                lanes = slice(128 * p, 128 * p + 128)
                q2 = twice(q_s[rows, lanes])
                kk = k_s[keys, lanes]
                g2 = twice(gctx[rows, lanes])
                s = nt(q2, kk) + bias
                prob = jnp.exp(s - lse[p, blk(i, 2 * QB), :])
                dp = nt(g2, v_s[keys, lanes])
                inner = jnp.sum(prob * dp, axis=1, keepdims=True)
                ds = (prob * (dp - inner)).astype(BF)
                dq[rows, lanes] = fold(nn(ds, kk)) * 0.125
                dk[keys, lanes] += tn(ds, q2)
                dv[keys, lanes] += tn(prob.astype(BF), g2)

        @pl.loop(0, Z)
        def _(c):
            rows = blk(c, LOC)
            for p in range(PAIRS):
                lanes = slice(128 * p, 128 * p + 128)
                dqkv[rows, lanes] = rotate(dq[rows, lanes], rows, -1.0).astype(BF)
                dqkv[rows, 256 + 128 * p : 384 + 128 * p] = rotate(
                    dk[rows, lanes], rows, -1.0
                ).astype(BF)
            dqkv[rows, 512:] = dv[rows, :].astype(BF)
            sums = jnp.sum(dqkv[rows, :].astype(F32), axis=0, keepdims=True)
            for s in range(3):
                vsum[4 + s : 5 + s, blk(z, 256)] += sums[:, 256 * s : 256 * s + 256]

        s_out.finish()
        outputs[...] = own[...].astype(BF)
        flush()

        @pl.loop(0, Z)
        def _(j):
            c = lax.rem(z + 1 + j, Z)
            rows = blk(c, LOC)
            g32[...] = nt(dqkv[rows, :], wqkv[...])
            h32[...] = nt(dhid[rows, :], wup[...])

            def back(i, carry):
                at = pl.ds(pl.multiple_of(c * LOC + i * 16, 16), 16)
                here = blk(i, 16)
                xhat = (x_all[at, :].astype(F32) - mean_s[at, :]) * rstd_s[at, :]
                ga, gm = g32[here, :], h32[here, :]
                for k, v in enumerate((ga * xhat, ga, gm * xhat, gm)):
                    acc[k] += v[:8] + v[8:]
                g32[here, :] = ga * gain_a + gm * gain_m
                return carry

            lax.fori_loop(0, LOC // 16, back, 0)

            @pl.when(j < Z - 1)
            def _():
                part[rows, :] = g32[...].astype(BF)

            @pl.when(j == Z - 1)
            def _():
                own[...] = g32[...]

        for k in range(4):
            vsum[k : k + 1, :] = jnp.sum(acc[k], axis=0, keepdims=True)
        s_in = Scatter(1)
        s_in.send()

        @pl.loop(0, Z)
        def _(c):
            g_qkv[c] = tn(attn_n[:, blk(c, 256)], dqkv[...]).astype(BF)
            g_up[c] = tn(mlp_n[:, blk(c, 256)], dhid[...]).astype(BF)

        s_in.relay()

        def add_og(i, carry):
            return carry + og_all[pl.ds(pl.multiple_of(z * LOC + i * 16, 16), 16), :].astype(F32)

        vsum[11:12, :] = jnp.sum(
            lax.fori_loop(0, LOC // 16, add_og, jnp.zeros((16, 1024), F32)), axis=0, keepdims=True
        )

    if stage >= 4:
        class Stream:
            def __init__(self, order, grad, temp, final, to_z=None):
                self.order, self.idx = order, index_of(order)
                self.grad, self.temp, self.final, self.to_z = grad, temp, final, to_z
                self.v = recvs.take(bits)
                self.g = recvs.take(nb)
                self.first, self.size, self.off = 0, chunks, 0

            def halve(self, k):
                if k < nb:
                    self.size //= 2
                    b = self.order[k]
                    mine = self.first + bit_of(r, b) * self.size
                    other = self.first + (1 - bit_of(r, b)) * self.size
                else:
                    b, mine, other = k, self.first, self.first
                self.mine = mine
                self.at = len(pending)
                go(
                    self.grad(other, self.size),
                    self.temp(self.off, self.size),
                    sends.take(1),
                    self.v + k,
                    (flip(r, b), z),
                )

            def add(self, k):
                got = self.temp(self.off, self.size)
                arrived(got, self.v + k)
                keep = self.grad(self.mine, self.size)
                if k >= nb:
                    pending[self.at][0].wait_send()
                    pending[self.at] = None
                n = keep.shape[-2] // 16
                for i in range(keep.shape[0] if len(keep.shape) == 3 else 1):
                    a, c = (keep.at[i], got.at[i]) if len(keep.shape) == 3 else (keep, got)

                    def step(j, carry):
                        a[blk(j, 16), :] = a[blk(j, 16), :] + c[blk(j, 16), :]
                        return carry

                    lax.fori_loop(0, n, step, 0)
                self.off += self.size
                self.first = self.mine

            def place(self):
                if self.to_z is None:
                    self.own = [local(self.grad(self.idx, 1), self.final(self.idx, 1))]
                    return
                self.zv = [recvs.take(Z) for _ in self.to_z]
                self.own = []
                for v, (src, dst) in zip(self.zv, self.to_z):
                    for step in (1, 3, 2):
                        t = lax.rem(z + step, Z)
                        go(src(t, self.idx), dst(z, self.idx), sends.take(1), v + z, (r, t))
                    self.own.append(local(src(z, self.idx), dst(z, self.idx)))

            def placed(self):
                if self.to_z is not None:
                    for v, (src, dst) in zip(self.zv, self.to_z):
                        for step in (1, 3, 2):
                            t = lax.rem(z + step, Z)
                            arrived(dst(t, self.idx), v + t)
                for copy in self.own:
                    copy.wait()

            def gather(self, k):
                size = 1 << k
                first = lax.div(self.idx, size) * size
                go(
                    self.final(first, size),
                    self.final(first, size),
                    sends.take(1),
                    self.g + k,
                    (flip(r, self.order[nb - 1 - k]), z),
                )

            def gathered(self, k):
                size = 1 << k
                first = flip(lax.div(self.idx, size), 0) * size
                arrived(self.final(first, size), self.g + k)

        def rows_of(ref, unit, lanes=slice(None)):
            def region(first, n):
                return ref.at[pl.ds(pl.multiple_of(first * unit, unit), n * unit), lanes]

            return region

        def deep_rows(ref):
            def region(first, n):
                return ref.at[:, pl.ds(pl.multiple_of(first * cr, cr), n * cr), :]

            return region

        def z_rows(ref, width, lanes):
            def src(t, idx):
                return ref.at[t, pl.ds(pl.multiple_of(idx * cr, cr), cr), lanes]

            return src

        def z_cols(ref, first, width):
            def dst(t, idx):
                return ref.at[
                    pl.ds(pl.multiple_of(idx * cr, cr), cr),
                    pl.ds(pl.multiple_of(first + t * width, width), width),
                ]

            return dst

        cd = FF // Z // chunks
        left, right = pl.ds(0, 512), pl.ds(512, 512)
        streams = [
            Stream(order_a, rows_of(g_down, cd, left), rows_of(t_down, cd, left), rows_of(f_down, cd, left)),
            Stream(order_b, rows_of(g_down, cd, right), rows_of(t_down, cd, right), rows_of(f_down, cd, right)),
            Stream(order_a, rows_of(g_out, cr), rows_of(t_out, cr), rows_of(f_out, cr)),
            Stream(
                order_b,
                deep_rows(g_up),
                deep_rows(t_up),
                rows_of(f_up, cr),
                [(z_rows(g_up, 1024, slice(None)), z_cols(f_up, 0, 1024))],
            ),
            Stream(
                order_a,
                deep_rows(g_qkv),
                deep_rows(t_qkv),
                rows_of(f_qkv, cr),
                [
                    (z_rows(g_qkv, 256, pl.ds(256 * s, 256)), z_cols(f_qkv, D * s, 256))
                    for s in range(3)
                ],
            ),
        ]
        vec_steps = [(0, b) for b in range(bits)] + [(1, b) for b in range(2)]
        vec_v2 = recvs.take(len(vec_steps))

        def vec_start(i):
            axis, b = vec_steps[i]
            dev = (flip(r, b), z) if axis == 0 else (r, flip(z, b))
            go(vsum, vrecv.at[i], sends.take(1), vec_v2 + i, dev)

        def vec_end(i):
            arrived(vrecv.at[i], vec_v2 + i)
            pending[-1][0].wait_send()
            pending.pop()
            vsum[...] = vsum[...] + vrecv[i]

        for k in range(bits):
            for s in streams:
                s.halve(k)
            for s in streams:
                s.add(k)
        s_in.finish()
        here = blk(z, LOC)

        def finish(i, carry):
            rows = blk(i, 16)
            at = pl.ds(pl.multiple_of(z * LOC + i * 16, 16), 16)
            rstd = rstd_s[at, :]
            xhat = (x_all[at, :].astype(F32) - mean_s[at, :]) * rstd
            g = own[rows, :]
            m1 = jnp.mean(g, axis=1, keepdims=True)
            m2 = jnp.mean(g * xhat, axis=1, keepdims=True)
            res = rstd * (g - m1 - xhat * m2)
            in_grad[rows, :] = (og_all[at, :].astype(F32) + res).astype(BF)
            return carry

        for s in streams:
            s.place()
        lax.fori_loop(0, LOC // 16, finish, 0)
        for s in streams:
            s.placed()
        for k in range(nb):
            for s in streams:
                s.gather(k)
            for s in streams:
                s.gathered(k)
        flush()
        for i in range(len(vec_steps)):
            vec_start(i)
            vec_end(i)
        vec_out[...] = vsum[...]

    flush()


def shards(
    replicas,
    stage,
    inputs,
    out_grad,
    segment_ids,
    ln_gain_attn,
    ln_bias_attn,
    ln_gain_mlp,
    ln_bias_mlp,
    qkv_weight,
    qkv_bias,
    out_weight,
    up_weight,
    up_bias,
    down_weight,
    output_bias,
    probe=(),
):
    z = lax.axis_index("shard")
    seg = segment_ids[0]
    count0 = jnp.sum((seg == 0).astype(jnp.int32))
    count1 = jnp.sum((seg <= 1).astype(jnp.int32))
    start = jnp.where(seg == 0, 0, jnp.where(seg == 1, count0, count1))
    position = (jnp.arange(TOK, dtype=jnp.int32) - start).astype(F32)
    half = ROT // 2
    freq = 1.0 / 10000.0 ** (jnp.arange(half, dtype=F32) * 2.0 / ROT)
    angles = position[:, None] * freq
    cosine, sine = jnp.cos(angles), jnp.sin(angles)
    pad1 = jnp.ones((TOK, HEAD - ROT), F32)
    pad0 = jnp.zeros((TOK, HEAD - ROT), F32)
    none = jnp.zeros((TOK, half), F32)
    tab_c = jnp.tile(jnp.concatenate([cosine, cosine, pad1], axis=1), (1, 2))
    tab_a = jnp.tile(jnp.concatenate([-sine, none, pad0], axis=1), (1, 2))
    tab_b = jnp.tile(jnp.concatenate([none, sine, pad0], axis=1), (1, 2))
    vec = jnp.concatenate(
        [
            ln_gain_attn,
            ln_bias_attn,
            ln_gain_mlp,
            ln_bias_mlp,
            qkv_bias,
            output_bias,
            jnp.zeros((8 * 256,), BF),
        ]
    ).reshape(16, 256)
    upb = up_bias.astype(F32).reshape(1, 1024)

    bits = int(math.log2(replicas))
    vm = pl.BlockSpec(memory_space=pltpu.VMEM)
    hbm = pl.BlockSpec(memory_space=pl.ANY)

    def v(*shape, dtype=BF):
        return pltpu.VMEM(shape, dtype)

    scratch = dict(
        x_all=v(TOK, D),
        og_all=v(TOK, D),
        vec_all=v(64, 256),
        wqkv=v(D, 768),
        wup=v(D, 1024),
        wout=v(256, D),
        wdown=v(1024, D),
        attn_n=v(TOK, D),
        mlp_n=v(TOK, D),
        mean_s=v(TOK, 1, dtype=F32),
        rstd_s=v(TOK, 1, dtype=F32),
        q_s=v(TOK, 256),
        k_s=v(TOK, 256),
        v_s=v(TOK, 256),
        ctx=v(TOK, 256),
        lse=v(PAIRS, 2 * TOK, 1, dtype=F32),
        h32=v(LOC, 1024, dtype=F32),
        g32=v(LOC, 1024, dtype=F32),
        acc=v(4, 8, 1024, dtype=F32),
        hidden=v(TOK, 1024),
        dgelu=v(TOK, 1024),
        part=v(TOK, D),
        own=v(LOC, D, dtype=F32),
        zrecv=v(2 * TOK, D),
        zrelay=v(2 * LOC, D),
        gctx=v(TOK, 256),
        dq=v(TOK, 256, dtype=F32),
        dk=v(TOK, 256, dtype=F32),
        dv=v(TOK, 256, dtype=F32),
        dqkv=v(TOK, 768),
        g_qkv=v(Z, 256, 768),
        g_up=v(Z, 256, 1024),
        g_out=v(256, D),
        g_down=v(1024, D),
        t_qkv=v(Z, 256, 768),
        t_up=v(Z, 256, 1024),
        t_out=v(256, D),
        t_down=v(1024, D),
        vsum=v(16, 1024, dtype=F32),
        vrecv=v(bits + 2, 16, 1024, dtype=F32),
        ssem=pltpu.SemaphoreType.DMA((NSEM,)),
        rsem=pltpu.SemaphoreType.DMA((NSEM,)),
        lsem=pltpu.SemaphoreType.DMA((32,)),
    )
    out_shape = [
        jax.ShapeDtypeStruct((LOC, D), BF),
        jax.ShapeDtypeStruct((LOC, D), BF),
        jax.ShapeDtypeStruct((256, 3 * D), BF),
        jax.ShapeDtypeStruct((256, FF), BF),
        jax.ShapeDtypeStruct((256, D), BF),
        jax.ShapeDtypeStruct((1024, D), BF),
        jax.ShapeDtypeStruct((16, 1024), F32),
    ]
    out_specs = [vm, vm, hbm, hbm, hbm, hbm, vm]
    names = list(scratch)
    extra = [jax.ShapeDtypeStruct(scratch[n].shape, scratch[n].dtype) for n in probe]

    def body(*refs):
        ins, rest = refs[:12], refs[12:]
        outs, rest = rest[: len(out_shape)], rest[len(out_shape) :]
        dumps, held = rest[: len(extra)], rest[len(extra) :]
        layer(replicas, stage, *ins, *outs, **dict(zip(names, held)))
        if probe:

            def run(sem):
                for n, d in zip(probe, dumps):
                    copy = pltpu.make_async_copy(held[names.index(n)], d, sem)
                    copy.start()
                    copy.wait()

            pl.run_scoped(run, pltpu.SemaphoreType.DMA)

    res = pl.pallas_call(
        body,
        out_shape=out_shape + extra,
        in_specs=[vm] + [hbm] * 6 + [vm] * 5,
        out_specs=out_specs + [hbm] * len(extra),
        scratch_shapes=list(scratch.values()),
        compiler_params=pltpu.CompilerParams(
            collective_id=0,
            has_side_effects=True,
            vmem_limit_bytes=62 * 2**20,
        ),
    )(
        inputs.reshape(LOC, D),
        out_grad.reshape(LOC, D),
        qkv_weight,
        up_weight,
        out_weight,
        down_weight,
        vec,
        upb,
        start.reshape(TOK, 1),
        tab_c,
        tab_a,
        tab_b,
    )
    outputs, in_grad, f_qkv, f_up, f_out, f_down, vec_out = res[:7]

    def cut(first, n):
        return lax.dynamic_slice_in_dim(first, z * n, n, 0)

    final = (
        outputs.reshape(1, LOC, D),
        in_grad.reshape(1, LOC, D),
        cut(vec_out[0], 256),
        cut(vec_out[1], 256),
        cut(vec_out[2], 256),
        cut(vec_out[3], 256),
        f_qkv.astype(F32),
        cut(vec_out[4:7].reshape(3072), 768),
        f_out.astype(F32),
        f_up.astype(F32),
        cut(vec_out[7:11].reshape(4096), 1024),
        f_down.astype(F32),
        cut(vec_out[11], 256),
    )
    return final + tuple(r[None, None] for r in res[7:]) if probe else final


def solution(mesh, stage=STAGE, probe=()):
    seq = P("replica", "shard", None)
    row = P("shard", None)
    one = P("shard")
    return jax.shard_map(
        partial(shards, mesh.shape["replica"], stage, probe=probe),
        mesh=mesh,
        in_specs=(seq, seq, P("replica", None), one, one, one, one, row, one, row, row, one, row, one),
        out_specs=(seq, seq, one, one, one, one, row, one, row, row, one, row, one)
        + tuple(P("replica", "shard") for _ in probe),
        check_vma=False,
    )
```

```python
import math
from functools import partial

import jax
import jax.numpy as jnp
from jax import lax
from jax.experimental import pallas as pl
from jax.experimental.pallas import tpu as pltpu
from jax.sharding import PartitionSpec as P

D = 1024
FF = 4096
HEADS = 16
HEAD = 64
ROT = 16
Z = 4
LOC = 256
TOK = 1024
PAIRS = 2
QB = 128
KB = 640
EPS = 1e-05
BF = jnp.bfloat16
F32 = jnp.float32
MESH = pl.DeviceIdType.MESH
NSEM = 256
SUB = 2


def bit_of(value, place):
    return lax.rem(lax.div(value, 1 << place), 2)


def flip(value, place):
    return value + (1 - 2 * bit_of(value, place)) * (1 << place)


def nn(a, b):
    return jnp.dot(a, b, preferred_element_type=F32)


def nt(a, b):
    return lax.dot_general(a, b, (((1,), (1,)), ((), ())), preferred_element_type=F32)


def tn(a, b):
    return lax.dot_general(a, b, (((0,), (0,)), ((), ())), preferred_element_type=F32)


def blk(i, n):
    return pl.ds(pl.multiple_of(i * n, n), n)


class Count:
    def __init__(self):
        self.used = 0

    def take(self, n):
        first = self.used
        self.used += n
        assert self.used <= NSEM
        return first


def layer(
    replicas,
    x_in,
    og_in,
    qkv_w,
    up_w,
    out_w,
    down_w,
    vec_in,
    tab_in,
    outputs,
    in_grad,
    f_qkv,
    f_up,
    f_out,
    f_down,
    vec_out,
    x_all,
    og_all,
    vec_all,
    tab,
    tab_c,
    tab_a,
    tab_b,
    start,
    wqkv,
    wup,
    wout,
    wdown,
    attn_n,
    mlp_n,
    mean_s,
    rstd_s,
    q_s,
    k_s,
    v_s,
    ctx,
    lse,
    h32,
    g32,
    acc,
    hidden,
    dgelu,
    part_o,
    part_i,
    own_o,
    own_i,
    land_o,
    land_i,
    gctx,
    dq,
    dk,
    dv,
    dqkv,
    g_qkv,
    g_up,
    g_out,
    g_down,
    t_qkv,
    t_up,
    t_out,
    t_down,
    vsum,
    vrecv,
    ssem,
    rsem,
    lsem,
):
    r = lax.axis_index("replica")
    z = lax.axis_index("shard")
    bits = int(math.log2(replicas))
    nb = min(bits, 4)
    chunks = 1 << nb
    sends, recvs, locals_ = Count(), Count(), Count()
    pending = []

    middle = (z == 1) | (z == 2)
    ends = (z == 0) | (z == 3)
    low = z < 2
    end = jnp.where(low, 0, 3)
    mid = jnp.where(low, 1, 2)
    other = 3 - mid
    far = 3 - end
    beside = z + 1 - 2 * lax.rem(z, 2)
    c1, c2, c3 = beside, other, far
    own_rows = blk(z, LOC)

    def remote(src, dst, s, v, dev):
        return pltpu.make_async_remote_copy(
            src_ref=src,
            dst_ref=dst,
            send_sem=ssem.at[s],
            recv_sem=rsem.at[v],
            device_id=dev,
            device_id_type=MESH,
        )

    def go(src, dst, s, v, dev, when=None):
        copy = remote(src, dst, s, v, dev)
        if when is None:
            copy.start()
        else:
            pl.when(when)(copy.start)
        pending.append((copy, when))

    def arrived(dst, v, when=None):
        copy = remote(dst, dst, 0, v, (r, z))
        if when is None:
            copy.wait_recv()
        else:
            pl.when(when)(copy.wait_recv)

    def local(src, dst):
        copy = pltpu.make_async_copy(src, dst, lsem.at[locals_.take(1)])
        copy.start()
        return copy

    def rows_at(first, n):
        return pl.ds(pl.multiple_of(first, n), n)

    vec_own = local(vec_in, vec_all.at[blk(z, 16)])
    tab_own = local(tab_in, tab)
    x_own = local(x_in, x_all.at[own_rows])

    barrier = pltpu.get_barrier_semaphore()
    for step in range(1, Z):
        pl.semaphore_signal(
            barrier, inc=1, device_id=(r, lax.rem(z + step, Z)), device_id_type=MESH
        )
    for b in range(bits):
        pl.semaphore_signal(barrier, inc=1, device_id=(flip(r, b), z), device_id_type=MESH)
    pl.semaphore_wait(barrier, Z - 1 + bits)

    order_a = list(range(nb))
    order_b = [0, *reversed(range(1, nb))]

    def index_of(order):
        return sum(bit_of(r, b) * (1 << (nb - 1 - k)) for k, b in enumerate(order))

    idx_a, idx_b = index_of(order_a), index_of(order_b)
    cr = LOC // chunks

    up_v, qkv_v, vec_v = recvs.take(Z), recvs.take(3 * Z), recvs.take(Z)
    for step in (1, 3, 2):
        t = lax.rem(z + step, Z)
        go(vec_in, vec_all.at[blk(z, 16)], sends.take(1), vec_v + z, (r, t))
    for step in (1, 3, 2):
        t = lax.rem(z + step, Z)
        go(
            up_w.at[blk(idx_a, cr), blk(t, 1024)],
            wup.at[rows_at(z * LOC + idx_a * cr, cr)],
            sends.take(1),
            up_v + z,
            (r, t),
        )
        for s in range(3):
            go(
                qkv_w.at[blk(idx_b, cr), rows_at(s * D + t * 256, 256)],
                wqkv.at[rows_at(z * LOC + idx_b * cr, cr), pl.ds(s * 256, 256)],
                sends.take(1),
                qkv_v + z * 3 + s,
                (r, t),
            )

    piece = LOC // SUB

    class Gather:
        def __init__(self, src, buf):
            self.src, self.buf = src, buf
            self.v = recvs.take(Z * SUB)

        def rows(self, c, k):
            return self.buf.at[rows_at(c * LOC + k * piece, piece)]

        def send(self):
            for k in range(SUB):
                for dev, when in ((mid, ends), (end, middle), (other, middle)):
                    go(
                        self.src.at[pl.ds(k * piece, piece)],
                        self.rows(z, k),
                        sends.take(1),
                        self.v + z * SUB + k,
                        (r, dev),
                        when,
                    )

        def hand(self, c, dev):
            for k in range(SUB):
                arrived(self.rows(c, k), self.v + c * SUB + k, middle)
                go(
                    self.rows(c, k),
                    self.rows(c, k),
                    sends.take(1),
                    self.v + c * SUB + k,
                    (r, dev),
                    middle,
                )

        def wait(self, c):
            for k in range(SUB):
                arrived(self.rows(c, k), self.v + c * SUB + k, ends)

    gx, gg = Gather(x_in, x_all), Gather(og_in, og_all)
    gx.send()
    own_up = local(up_w.at[:, blk(z, 1024)], wup.at[own_rows])
    own_qkv = [
        local(qkv_w.at[:, rows_at(s * D + z * 256, 256)], wqkv.at[own_rows, pl.ds(s * 256, 256)])
        for s in range(3)
    ]
    og_own = local(og_in, og_all.at[own_rows])
    w_own = [local(out_w, wout), local(down_w, wdown)]

    ag_v = recvs.take(3 * 2 * nb)

    def weight_region(kind, zz, first, n):
        ref = wup if kind == 0 else wqkv
        return ref.at[pl.ds(pl.multiple_of(zz * LOC + first * cr, cr), n * cr)]

    def weight_step(k):
        for j in range(1, Z):
            zz = lax.rem(z + j, Z)
            for kind, order, idx in ((0, order_a, idx_a), (1, order_b, idx_b)):
                b = order[nb - 1 - k]
                size = 1 << k
                first = lax.div(idx, size) * size
                go(
                    weight_region(kind, zz, first, size),
                    weight_region(kind, zz, first, size),
                    sends.take(1),
                    ag_v + ((j - 1) * 2 + kind) * nb + k,
                    (flip(r, b), z),
                )

    def weight_wait(k):
        for j in range(1, Z):
            zz = lax.rem(z + j, Z)
            for kind, idx in ((0, idx_a), (1, idx_b)):
                size = 1 << k
                first = flip(lax.div(idx, size), 0) * size
                arrived(weight_region(kind, zz, first, size), ag_v + ((j - 1) * 2 + kind) * nb + k)

    tab_own.wait()
    vec_own.wait()
    x_own.wait()
    own_up.wait()
    og_own.wait()
    for copy in own_qkv + w_own:
        copy.wait()
    lane = lax.broadcasted_iota(jnp.int32, (QB, 128), 1)
    turned = lax.rem(lane, HEAD) < ROT

    @pl.loop(0, TOK // 128)
    def _(i):
        at = blk(i, 128)
        cosine, sine, first = tab[0:8, at], tab[8:16, at], tab[16:24, at]
        none = jnp.zeros_like(cosine)
        half = [cosine, cosine, -sine, none, none, sine, first, none]
        wide = jnp.concatenate(half + half, axis=0).T
        tab_c[at, :] = jnp.where(turned, wide, 1.0)
        tab_a[at, :] = jnp.where(turned, pltpu.roll(wide, 112, 1), 0.0)
        tab_b[at, :] = jnp.where(turned, pltpu.roll(wide, 96, 1), 0.0)
        start[at, :] = wide[:, 48:49]

    for j in range(1, Z):
        zz = lax.rem(z + j, Z)
        arrived(vec_all.at[blk(zz, 16)], vec_v + zz)

    def vector(row):
        return jnp.concatenate(
            [vec_all[16 * c : 16 * c + 16, :][row : row + 1, :] for c in range(Z)], axis=1
        ).astype(F32)

    def vector256(i):
        block = vec_all[blk(lax.div(i, 3), 16), :].astype(F32)
        rows = lax.broadcasted_iota(jnp.int32, (16, 256), 0)
        return jnp.sum(jnp.where(rows == 4 + lax.rem(i, 3), block, 0.0), axis=0, keepdims=True)

    gain_a, bias_a, gain_m, bias_m, bias_o = [vector(i) for i in (0, 1, 2, 3, 7)]
    qkv_b = [vector256(s * Z + z) for s in range(3)]
    mine = vec_all[blk(z, 16), :]
    up_shift = jnp.concatenate([mine[8 + i : 9 + i, :] for i in range(4)], axis=1).astype(F32)

    def norm_rows(c):
        def norm(i, carry):
            rows = rows_at(c * LOC + i * 16, 16)
            v = x_all[rows, :].astype(F32)
            mean = jnp.mean(v, axis=1, keepdims=True)
            cen = v - mean
            rstd = lax.rsqrt(jnp.mean(cen * cen, axis=1, keepdims=True) + EPS)
            xhat = cen * rstd
            attn_n[rows, :] = (xhat * gain_a + bias_a).astype(BF)
            mlp_n[rows, :] = (xhat * gain_m + bias_m).astype(BF)
            mean_s[rows, :] = mean
            rstd_s[rows, :] = rstd
            return carry

        lax.fori_loop(0, LOC // 16, norm, 0, unroll=2)

    def rotate(t, rows, sign):
        return (
            t * tab_c[rows, :]
            + sign * (pltpu.roll(t, 120, 1) * tab_a[rows, :])
            + sign * (pltpu.roll(t, 8, 1) * tab_b[rows, :])
        )

    def project(c):
        rows = blk(c, LOC)
        res = nn(attn_n[rows, :], wqkv[...])
        for p in range(PAIRS):
            lanes = slice(128 * p, 128 * p + 128)
            t = res[:, lanes] + qkv_b[0][:, lanes]
            q_s[rows, lanes] = (rotate(t, rows, 1.0) * 0.125).astype(BF)
            t = res[:, 256 + 128 * p : 384 + 128 * p] + qkv_b[1][:, lanes]
            k_s[rows, lanes] = rotate(t, rows, 1.0).astype(BF)
        v_s[rows, :] = (res[:, 512:] + qkv_b[2]).astype(BF)
        h32[...] = nn(mlp_n[rows, :], wup[...])

        def act(i, carry):
            v = h32[blk(i, 16), :] + up_shift
            cdf = 0.5 + 0.5 * lax.erf(v * (0.5**0.5))
            at = rows_at(c * LOC + i * 16, 16)
            hidden[at, :] = (v * cdf).astype(BF)
            dgelu[at, :] = (
                cdf + v * jnp.exp(-0.5 * v * v) * (1.0 / math.sqrt(2.0 * math.pi))
            ).astype(BF)
            return carry

        lax.fori_loop(0, LOC // 16, act, 0)

    def twice(t):
        zero = jnp.zeros_like(t)
        return jnp.concatenate(
            [jnp.where(lane < HEAD, t, zero), jnp.where(lane >= HEAD, t, zero)], axis=0
        )

    def fold(t):
        return jnp.where(lane < HEAD, t[:QB], t[QB:])

    def window(i):
        first = pl.multiple_of(jnp.maximum(i * QB - (KB - QB), 0), QB)
        at = first + lax.broadcasted_iota(jnp.int32, (QB, KB), 1)
        row = i * QB + lax.broadcasted_iota(jnp.int32, (QB, KB), 0)
        ok = (at <= row) & (at.astype(F32) >= start[blk(i, QB), :])
        bias = jnp.where(ok, 0.0, -1e30)
        return pl.ds(first, KB), jnp.concatenate([bias, bias], axis=0)

    def attend(c):
        @pl.loop(0, LOC // QB)
        def _(j):
            i = c * (LOC // QB) + j
            keys, bias = window(i)
            rows = blk(i, QB)
            for p in range(PAIRS):
                lanes = slice(128 * p, 128 * p + 128)
                s = nt(twice(q_s[rows, lanes]), k_s[keys, lanes]) + bias
                top = jnp.max(s, axis=1, keepdims=True)
                e = jnp.exp(s - top)
                total = jnp.sum(e, axis=1, keepdims=True)
                lse[p, blk(i, 2 * QB), :] = top + jnp.log(total)
                prob = (e * (1.0 / total)).astype(BF)
                ctx[rows, lanes] = fold(nn(prob, v_s[keys, lanes])).astype(BF)

    class Scatter:
        def __init__(self, part, own, land):
            self.part, self.own, self.land = part, own, land
            self.v = recvs.take(5 * SUB)

        def slot(self, s, k):
            return self.land.at[rows_at(s * LOC + k * piece, piece)]

        def rows(self, c, k):
            return self.part.at[rows_at(c * LOC + k * piece, piece)]

        def send(self, c):
            place = jnp.clip(jnp.where(low, 3 - c, c), 0, 2)
            when = ends & (c != z)
            for k in range(SUB):
                go(
                    self.rows(c, k),
                    self.slot(place, k),
                    sends.take(1),
                    self.v + place * SUB + k,
                    (r, mid),
                    when,
                )

        def pass_on(self, came, c, dev, goes, when):
            for k in range(SUB):
                arrived(self.slot(came, k), self.v + came * SUB + k, when)

                @pl.when(when)
                def _():
                    def add(i, carry):
                        at = rows_at(c * LOC + k * piece + i * 16, 16)
                        got = rows_at(came * LOC + k * piece + i * 16, 16)
                        self.part[at, :] = self.part[at, :] + self.land[got, :]
                        return carry

                    lax.fori_loop(0, piece // 16, add, 0, unroll=2)

                go(
                    self.rows(c, k),
                    self.slot(goes, k),
                    sends.take(1),
                    self.v + goes * SUB + k,
                    (r, dev),
                    when,
                )

        def pass_far(self, when):
            self.pass_on(0, far, other, 3, when)

        def pass_other(self, when):
            self.pass_on(1, other, other, 4, when)

        def pass_end(self, when):
            self.pass_on(3, end, end, 0, when)

        def finish(self):
            for came, when in ((0, ends), (2, middle), (4, middle)):
                for k in range(SUB):
                    arrived(self.slot(came, k), self.v + came * SUB + k, when)

                @pl.when(when)
                def _():
                    def add(i, carry):
                        got = self.land[rows_at(came * LOC + i * 16, 16), :]
                        self.own[blk(i, 16), :] += got.astype(F32)
                        return carry

                    lax.fori_loop(0, LOC // 16, add, 0, unroll=2)

    s_out = Scatter(part_o, own_o, land_o)
    s_in = Scatter(part_i, own_i, land_i)

    def mix(c):
        rows = blk(c, LOC)
        res = nn(ctx[rows, :], wout[...]) + nn(hidden[rows, :], wdown[...])
        if c is z:
            own_o[...] = res + x_all[own_rows, :].astype(F32) + bias_o
        else:
            part_o[rows, :] = res.astype(BF)
            s_out.send(c)

    vsum[...] = jnp.zeros_like(vsum)
    acc[...] = jnp.zeros_like(acc)
    dk[...] = jnp.zeros_like(dk)
    dv[...] = jnp.zeros_like(dv)

    def side(c):
        rows = blk(c, LOC)
        gctx[rows, :] = nt(og_all[rows, :], wout[...]).astype(BF)
        h32[...] = nt(og_all[rows, :], wdown[...])

        def act(i, carry):
            at = rows_at(c * LOC + i * 16, 16)
            g = (h32[blk(i, 16), :] * dgelu[at, :].astype(F32)).astype(BF)
            dgelu[at, :] = g
            return carry + g.astype(F32)

        total = lax.fori_loop(0, LOC // 16, act, jnp.zeros((16, 1024), F32))
        vsum[pl.ds(7 + z, 1), :] += jnp.sum(total, axis=0, keepdims=True)

    dhid = dgelu

    def back(c):
        @pl.loop(0, LOC // QB)
        def _(j):
            i = c * (LOC // QB) + j
            keys, bias = window(i)
            rows = blk(i, QB)
            for p in range(PAIRS):
                lanes = slice(128 * p, 128 * p + 128)
                q2 = twice(q_s[rows, lanes])
                kk = k_s[keys, lanes]
                g2 = twice(gctx[rows, lanes])
                s = nt(q2, kk) + bias
                prob = jnp.exp(s - lse[p, blk(i, 2 * QB), :])
                dp = nt(g2, v_s[keys, lanes])
                inner = jnp.sum(prob * dp, axis=1, keepdims=True)
                ds = (prob * (dp - inner)).astype(BF)
                dq[rows, lanes] = fold(nn(ds, kk)) * 0.125
                dk[keys, lanes] += tn(ds, q2)
                dv[keys, lanes] += tn(prob.astype(BF), g2)

        rows = blk(c, LOC)
        for p in range(PAIRS):
            lanes = slice(128 * p, 128 * p + 128)
            dqkv[rows, lanes] = rotate(dq[rows, lanes], rows, -1.0).astype(BF)
            dqkv[rows, 256 + 128 * p : 384 + 128 * p] = rotate(dk[rows, lanes], rows, -1.0).astype(BF)
        dqkv[rows, 512:] = dv[rows, :].astype(BF)
        sums = jnp.sum(dqkv[rows, :].astype(F32), axis=0, keepdims=True)
        for s in range(3):
            vsum[4 + s : 5 + s, blk(z, 256)] += sums[:, 256 * s : 256 * s + 256]
        g32[...] = nt(dqkv[rows, :], wqkv[...])
        h32[...] = nt(dhid[rows, :], wup[...])

        def step(i, carry):
            at = rows_at(c * LOC + i * 16, 16)
            here = blk(i, 16)
            xhat = (x_all[at, :].astype(F32) - mean_s[at, :]) * rstd_s[at, :]
            ga, gm = g32[here, :], h32[here, :]
            for k, v in enumerate((ga * xhat, ga, gm * xhat, gm)):
                acc[k] += v[:8] + v[8:]
            g = ga * gain_a + gm * gain_m
            g32[here, :] = g
            part_i[at, :] = g.astype(BF)
            return carry

        lax.fori_loop(0, LOC // 16, step, 0)

        @pl.when(z == c)
        def _():
            own_i[...] = g32[...]

        s_in.send(c)

    class Stream:
        def __init__(self, order, grad, temp, final, across=None):
            self.order, self.idx = order, index_of(order)
            self.grad, self.temp, self.final, self.across = grad, temp, final, across
            self.v, self.g = recvs.take(bits), recvs.take(nb)
            self.zv = recvs.take(Z) if across else None
            self.first, self.size, self.off = 0, chunks, 0

        def halve(self, k):
            if k < nb:
                self.size //= 2
                b = self.order[k]
                keep = self.first + bit_of(r, b) * self.size
                give = self.first + (1 - bit_of(r, b)) * self.size
            else:
                b, keep, give = k, self.first, self.first
            self.keep = keep
            self.at = len(pending)
            go(
                self.grad(give, self.size),
                self.temp(self.off, self.size),
                sends.take(1),
                self.v + k,
                (flip(r, b), z),
            )

        def add(self, k):
            got = self.temp(self.off, self.size)
            arrived(got, self.v + k)
            keep = self.grad(self.keep, self.size)
            if k >= nb:
                pending[self.at][0].wait_send()
                pending[self.at] = None
            deep = len(keep.shape) == 3
            for i in range(keep.shape[0] if deep else 1):
                a, b = (keep.at[i], got.at[i]) if deep else (keep, got)

                def step(j, carry):
                    a[blk(j, 16), :] = a[blk(j, 16), :] + b[blk(j, 16), :]
                    return carry

                lax.fori_loop(0, keep.shape[-2] // 16, step, 0)
            self.off += self.size
            self.first = self.keep

        def place(self):
            if self.across is None:
                self.put = local(self.grad(self.idx, 1), self.final(self.idx, 1))
                return
            src, dst = self.across
            for step in (2, 1, 3):
                t = lax.rem(z + step, Z)
                go(src(t, self.idx), dst(z, self.idx), sends.take(1), self.zv + z, (r, t))
            self.put = local(src(z, self.idx), dst(z, self.idx))

        def placed(self):
            if self.across is not None:
                for step in (1, 3, 2):
                    t = lax.rem(z + step, Z)
                    arrived(self.across[1](t, self.idx), self.zv + t)
            self.put.wait()

        def gather(self, k):
            size = 1 << k
            first = lax.div(self.idx, size) * size
            go(
                self.final(first, size),
                self.final(first, size),
                sends.take(1),
                self.g + k,
                (flip(r, self.order[nb - 1 - k]), z),
            )

        def gathered(self, k):
            size = 1 << k
            first = flip(lax.div(self.idx, size), 0) * size
            arrived(self.final(first, size), self.g + k)

    def wide_rows(ref, unit, lanes):
        return lambda first, n: ref.at[pl.ds(pl.multiple_of(first * unit, unit), n * unit), lanes]

    def deep_rows(ref, lanes):
        return lambda first, n: ref.at[:, pl.ds(pl.multiple_of(first * cr, cr), n * cr), lanes]

    def deep_block(ref, lanes):
        return lambda t, idx: ref.at[t, rows_at(idx * cr, cr), lanes]

    cd = FF // Z // chunks

    def pair(grad, temp, final, unit, width):
        made = []
        for order, lanes in ((order_a, pl.ds(0, width)), (order_b, pl.ds(width, width))):
            if unit:
                refs = [wide_rows(ref, unit, lanes) for ref in (grad, temp, final)]
                made.append(Stream(order, *refs))
            else:
                refs = [deep_rows(ref, lanes) for ref in (grad, temp, final)]
                both = (deep_block(grad, lanes), deep_block(final, lanes))
                made.append(Stream(order, *refs, both))
        return made

    class Group:
        def __init__(self, streams):
            self.streams, self.at = streams, 0

        def all(self, name, *args):
            for s in self.streams:
                getattr(s, name)(*args)

        def go_on(self, times=1):
            for _ in range(times):
                n = self.at
                if 0 < n <= bits:
                    self.all("add", n - 1)
                if n < bits:
                    self.all("halve", n)
                elif n == bits:
                    self.all("place")
                elif n == bits + 1:
                    self.all("placed")
                else:
                    self.all("gathered", n - bits - 2)
                if bits + 1 <= n < bits + 1 + nb:
                    self.all("gather", n - bits - 1)
                self.at += 1

    down = Group(pair(g_down, t_down, f_down, cd, 512) + pair(g_out, t_out, f_out, cr, 512))
    up = Group(pair(g_up, t_up, f_up, 0, 512))
    qkv = Group(pair(g_qkv, t_qkv, f_qkv, 0, 384))
    total_steps = bits + 2 + nb

    vec_steps = [(0, b) for b in range(bits)] + [(1, b) for b in range(2)]
    vec_v2 = recvs.take(len(vec_steps))
    vec_at = [0]

    def vec_on():
        n = vec_at[0]
        if n > len(vec_steps):
            return
        if n > 0:
            arrived(vrecv.at[n - 1], vec_v2 + n - 1)
            pending[vec_at[1]][0].wait_send()
            pending[vec_at[1]] = None
            vsum[...] = vsum[...] + vrecv[n - 1]
        if n < len(vec_steps):
            axis, b = vec_steps[n]
            dev = (flip(r, b), z) if axis == 0 else (r, flip(z, b))
            vec_at[1:] = [len(pending)]
            go(vsum, vrecv.at[n], sends.take(1), vec_v2 + n, dev)
        vec_at[0] += 1

    norm_rows(z)
    for j in range(1, Z):
        zz = lax.rem(z + j, Z)
        arrived(weight_region(0, zz, idx_a, 1), up_v + zz)
        for s in range(3):
            arrived(
                wqkv.at[rows_at(zz * LOC + idx_b * cr, cr), pl.ds(s * 256, 256)],
                qkv_v + zz * 3 + s,
            )
    for k in range(nb):
        weight_step(k)
        if k == nb - 1:
            gx.hand(c1, other)
            gx.hand(c2, end)
            gx.wait(c1)
            norm_rows(c1)
        weight_wait(k)
    project(z)
    project(c1)
    gx.hand(c3, end)
    gx.wait(c2)
    norm_rows(c2)
    project(c2)
    gx.wait(c3)
    gg.send()
    norm_rows(c3)
    project(c3)
    attend(c3)
    mix(c3)
    attend(c2)
    mix(c2)
    gg.hand(c1, other)
    gg.hand(c2, end)
    attend(c1)
    mix(c1)
    attend(z)
    mix(z)
    side(z)
    gg.wait(c1)
    side(c1)
    gg.hand(c3, end)
    s_out.pass_far(middle)
    gg.wait(c2)
    side(c2)
    s_out.pass_other(middle)
    gg.wait(c3)
    side(c3)
    g_out[...] = tn(ctx[...], og_all[...]).astype(BF)

    @pl.loop(0, Z)
    def _(c):
        g_down[blk(c, 256), :] = tn(hidden[:, blk(c, 256)], og_all[...]).astype(BF)

    down.go_on()
    s_out.pass_end(middle)
    back(3)
    down.go_on()
    back(2)
    down.go_on()

    @pl.loop(0, Z)
    def _(c):
        g_up[c] = tn(mlp_n[:, blk(c, 256)], dhid[...]).astype(BF)

    up.go_on()
    s_out.finish()
    outputs[...] = own_o[...].astype(BF)
    back(1)
    down.go_on()
    up.go_on()
    s_in.pass_far(z == 1)
    s_in.pass_other(z == 1)
    back(0)
    down.go_on()
    up.go_on()
    s_in.pass_end(z == 2)

    @pl.loop(0, Z)
    def _(c):
        g_qkv[c] = tn(attn_n[:, blk(c, 256)], dqkv[...]).astype(BF)

    qkv.go_on()
    s_in.pass_other(z == 2)

    def add_og(i, carry):
        return carry + og_all[rows_at(z * LOC + i * 16, 16), :].astype(F32)

    vsum[11:12, :] = jnp.sum(
        lax.fori_loop(0, LOC // 16, add_og, jnp.zeros((16, 1024), F32)), axis=0, keepdims=True
    )
    for k in range(4):
        vsum[k : k + 1, :] = jnp.sum(acc[k], axis=0, keepdims=True)
    vec_on()
    down.go_on()
    up.go_on()
    qkv.go_on()
    s_in.pass_far(z == 2)
    vec_on()
    down.go_on()
    up.go_on()
    qkv.go_on()
    vec_on()
    while qkv.at < total_steps:
        if down.at < total_steps:
            down.go_on()
        if up.at < total_steps:
            up.go_on()
        qkv.go_on()
        if qkv.at == bits + 2:
            s_in.pass_end(z == 1)
        vec_on()
    while vec_at[0] <= len(vec_steps):
        vec_on()
    vec_out[...] = vsum[...]
    s_in.finish()

    def finish(i, carry):
        rows = blk(i, 16)
        at = rows_at(z * LOC + i * 16, 16)
        rstd = rstd_s[at, :]
        xhat = (x_all[at, :].astype(F32) - mean_s[at, :]) * rstd
        g = own_i[rows, :]
        m1 = jnp.mean(g, axis=1, keepdims=True)
        m2 = jnp.mean(g * xhat, axis=1, keepdims=True)
        res = rstd * (g - m1 - xhat * m2)
        in_grad[rows, :] = (og_all[at, :].astype(F32) + res).astype(BF)
        return carry

    lax.fori_loop(0, LOC // 16, finish, 0, unroll=2)
    for copy, when in [p for p in pending if p is not None]:
        if when is None:
            copy.wait_send()
        else:
            pl.when(when)(copy.wait_send)


def tail(outs_in, in_in, f_qkv, f_up, f_out, f_down, vec, *results):
    z = lax.axis_index("shard")
    outs, ingrad, gga, gba, ggm, gbm, gqkv, gqkvb, gout, gup, gupb, gdown, goutb = results
    outs[...] = outs_in[...]
    ingrad[...] = in_in[...]
    for t in range(Z):
        gup[:, 1024 * t : 1024 * t + 1024] = f_up[t].astype(F32)
        for s in range(3):
            first = D * s + 256 * t
            gqkv[:, first : first + 256] = f_qkv[t, :, 256 * s : 256 * s + 256].astype(F32)
    gout[...] = f_out[...].astype(F32)
    gdown[...] = f_down[...].astype(F32)

    @pl.when(pl.program_id(0) == 0)
    def _():
        for k, ref in ((0, gga), (1, gba), (2, ggm), (3, gbm), (11, goutb)):
            ref[...] = vec[k : k + 1, blk(z, 256)]
        for i in range(3):
            g = 3 * z + i
            gqkvb[:, 256 * i : 256 * i + 256] = vec[pl.ds(4 + lax.div(g, Z), 1), blk(lax.rem(g, Z), 256)]
        gupb[...] = vec[pl.ds(7 + z, 1), :]


def shards(
    replicas,
    inputs,
    out_grad,
    segment_ids,
    ln_gain_attn,
    ln_bias_attn,
    ln_gain_mlp,
    ln_bias_mlp,
    qkv_weight,
    qkv_bias,
    out_weight,
    up_weight,
    up_bias,
    down_weight,
    output_bias,
):
    seg = segment_ids
    count0 = jnp.sum((seg == 0).astype(jnp.int32))
    count1 = jnp.sum((seg <= 1).astype(jnp.int32))
    start = jnp.where(seg == 0, 0, jnp.where(seg == 1, count0, count1))
    position = (lax.broadcasted_iota(jnp.int32, (1, TOK), 1) - start).astype(F32)
    half = ROT // 2
    freq = 1.0 / 10000.0 ** (jnp.arange(half, dtype=F32) * 2.0 / ROT)
    angles = freq[:, None] * position
    tab = jnp.concatenate(
        [jnp.cos(angles), jnp.sin(angles), jnp.broadcast_to(start.astype(F32), (8, TOK))], axis=0
    )
    vec = jnp.concatenate(
        [
            v.reshape(-1, 256)
            for v in (
                ln_gain_attn,
                ln_bias_attn,
                ln_gain_mlp,
                ln_bias_mlp,
                qkv_bias,
                output_bias,
                up_bias,
                jnp.zeros((4 * 256,), BF),
            )
        ],
        axis=0,
    )
    bits = int(math.log2(replicas))
    vm = pl.BlockSpec(memory_space=pltpu.VMEM)
    hbm = pl.BlockSpec(memory_space=pl.ANY)

    def v(*shape, dtype=BF):
        return pltpu.VMEM(shape, dtype)

    scratch = dict(
        x_all=v(TOK, D),
        og_all=v(TOK, D),
        vec_all=v(64, 256),
        tab=v(24, TOK, dtype=F32),
        tab_c=v(TOK, 128, dtype=F32),
        tab_a=v(TOK, 128, dtype=F32),
        tab_b=v(TOK, 128, dtype=F32),
        start=v(TOK, 1, dtype=F32),
        wqkv=v(D, 768),
        wup=v(D, 1024),
        wout=v(256, D),
        wdown=v(1024, D),
        attn_n=v(TOK, D),
        mlp_n=v(TOK, D),
        mean_s=v(TOK, 1, dtype=F32),
        rstd_s=v(TOK, 1, dtype=F32),
        q_s=v(TOK, 256),
        k_s=v(TOK, 256),
        v_s=v(TOK, 256),
        ctx=v(TOK, 256),
        lse=v(PAIRS, 2 * TOK, 1, dtype=F32),
        h32=v(LOC, 1024, dtype=F32),
        g32=v(LOC, 1024, dtype=F32),
        acc=v(4, 8, 1024, dtype=F32),
        hidden=v(TOK, 1024),
        dgelu=v(TOK, 1024),
        part_o=v(TOK, D),
        part_i=v(TOK, D),
        own_o=v(LOC, D, dtype=F32),
        own_i=v(LOC, D, dtype=F32),
        land_o=v(5 * LOC, D),
        land_i=v(5 * LOC, D),
        gctx=v(TOK, 256),
        dq=v(TOK, 256, dtype=F32),
        dk=v(TOK, 256, dtype=F32),
        dv=v(TOK, 256, dtype=F32),
        dqkv=v(TOK, 768),
        g_qkv=v(Z, 256, 768),
        g_up=v(Z, 256, 1024),
        g_out=v(256, D),
        g_down=v(1024, D),
        t_qkv=v(Z, 256, 768),
        t_up=v(Z, 256, 1024),
        t_out=v(256, D),
        t_down=v(1024, D),
        vsum=v(16, 1024, dtype=F32),
        vrecv=v(bits + 2, 16, 1024, dtype=F32),
        ssem=pltpu.SemaphoreType.DMA((NSEM,)),
        rsem=pltpu.SemaphoreType.DMA((NSEM,)),
        lsem=pltpu.SemaphoreType.DMA((32,)),
    )
    names = list(scratch)

    def body(*refs):
        layer(replicas, *refs[:15], **dict(zip(names, refs[15:])))

    res = pl.pallas_call(
        body,
        out_shape=[
            jax.ShapeDtypeStruct((LOC, D), BF),
            jax.ShapeDtypeStruct((LOC, D), BF),
            jax.ShapeDtypeStruct((Z, 256, 768), BF),
            jax.ShapeDtypeStruct((Z, 256, 1024), BF),
            jax.ShapeDtypeStruct((256, D), BF),
            jax.ShapeDtypeStruct((1024, D), BF),
            jax.ShapeDtypeStruct((16, 1024), F32),
        ],
        in_specs=[hbm] * 8,
        out_specs=[vm, vm, hbm, hbm, hbm, hbm, vm],
        scratch_shapes=list(scratch.values()),
        compiler_params=pltpu.CompilerParams(
            collective_id=0,
            has_side_effects=True,
            vmem_limit_bytes=61 * 2**20,
        ),
    )(
        inputs.reshape(LOC, D),
        out_grad.reshape(LOC, D),
        qkv_weight,
        up_weight,
        out_weight,
        down_weight,
        vec,
        tab,
    )
    steps = 8
    n = LOC // steps
    row = pl.BlockSpec((n, D), lambda i: (i, 0))
    tall = pl.BlockSpec((1024 // steps, D), lambda i: (i, 0))

    def fixed(w):
        return pl.BlockSpec((1, w), lambda i: (0, 0))

    small, wide = [fixed(256)], [fixed(768)]
    final = pl.pallas_call(
        tail,
        grid=(steps,),
        in_specs=[
            row,
            row,
            pl.BlockSpec((Z, n, 768), lambda i: (0, i, 0)),
            pl.BlockSpec((Z, n, 1024), lambda i: (0, i, 0)),
            row,
            tall,
            pl.BlockSpec((16, 1024), lambda i: (0, 0)),
        ],
        out_specs=[row, row]
        + small * 4
        + [pl.BlockSpec((n, 3 * D), lambda i: (i, 0))]
        + wide
        + [row, pl.BlockSpec((n, FF), lambda i: (i, 0)), fixed(1024), tall]
        + small,
        out_shape=[jax.ShapeDtypeStruct((LOC, D), BF)] * 2
        + [jax.ShapeDtypeStruct((1, 256), F32)] * 4
        + [
            jax.ShapeDtypeStruct((256, 3 * D), F32),
            jax.ShapeDtypeStruct((1, 768), F32),
            jax.ShapeDtypeStruct((256, D), F32),
            jax.ShapeDtypeStruct((256, FF), F32),
            jax.ShapeDtypeStruct((1, 1024), F32),
            jax.ShapeDtypeStruct((1024, D), F32),
            jax.ShapeDtypeStruct((1, 256), F32),
        ],
    )(*res)
    shapes = [(1, LOC, D)] * 2 + [(256,)] * 4 + [None, (768,), None, None, (1024,), None, (256,)]
    return tuple(a if s is None else a.reshape(s) for a, s in zip(final, shapes))


def solution(mesh):
    seq = P("replica", "shard", None)
    row = P("shard", None)
    one = P("shard")
    return jax.shard_map(
        partial(shards, mesh.shape["replica"]),
        mesh=mesh,
        in_specs=(seq, seq, P("replica", None), one, one, one, one, row, one, row, row, one, row, one),
        out_specs=(seq, seq, one, one, one, one, row, one, row, row, one, row, one),
        check_vma=False,
    )
```

```python
import math
from functools import partial

import jax
import jax.numpy as jnp
import numpy as np
from jax import lax
from jax.experimental import pallas as pl
from jax.experimental.pallas import tpu as pltpu
from jax.sharding import PartitionSpec as P

D = 1024
FF = 4096
HEADS = 16
HEAD = 64
ROT = 16
Z = 4
LOC = 256
TOK = 1024
PAIRS = 2
QB = 128
KB = 640
EPS = 1e-05
BF = jnp.bfloat16
F32 = jnp.float32
MESH = pl.DeviceIdType.MESH
NSEM = 256
SUB = 2


def bit_of(value, place):
    return lax.rem(lax.div(value, 1 << place), 2)


def flip(value, place):
    return value + (1 - 2 * bit_of(value, place)) * (1 << place)


def nn(a, b):
    return jnp.dot(a, b, preferred_element_type=F32)


def nt(a, b):
    return lax.dot_general(a, b, (((1,), (1,)), ((), ())), preferred_element_type=F32)


def tn(a, b):
    return lax.dot_general(a, b, (((0,), (0,)), ((), ())), preferred_element_type=F32)


def blk(i, n):
    return pl.ds(pl.multiple_of(i * n, n), n)


class Count:
    def __init__(self):
        self.used = 0

    def take(self, n):
        first = self.used
        self.used += n
        assert self.used <= NSEM
        return first


def layer(
    replicas,
    x_in,
    og_in,
    qkv_w,
    up_w,
    out_w,
    down_w,
    gain_a_in,
    bias_a_in,
    gain_m_in,
    bias_m_in,
    bias_o_in,
    qkv_b_in,
    up_b_in,
    seg_in,
    outputs,
    in_grad,
    f_qkv,
    f_up,
    f_od,
    vec_out,
    x_all,
    og_all,
    gain_a_all,
    bias_a_all,
    gain_m_all,
    bias_m_all,
    bias_o_all,
    qkv_b_all,
    up_b,
    seg,
    tab_c,
    tab_a,
    tab_b,
    start,
    wqkv,
    wup,
    wout,
    wdown,
    attn_n,
    mlp_n,
    mean_s,
    rstd_s,
    q_s,
    k_s,
    v_s,
    ctx,
    lse,
    h32,
    g32,
    acc,
    hidden,
    dgelu,
    part_o,
    part_i,
    own_o,
    own_i,
    land_o,
    land_i,
    gctx,
    dq,
    dk,
    dv,
    dqkv,
    g_qkv,
    g_up,
    g_od,
    t_qkv,
    t_up,
    t_od,
    vsum,
    vrecv,
    ssem,
    rsem,
    lsem,
):
    r = lax.axis_index("replica")
    z = lax.axis_index("shard")
    bits = int(math.log2(replicas))
    nb = min(bits, 4)
    chunks = 1 << nb
    sends, recvs, locals_ = Count(), Count(), Count()
    pending = []

    middle = (z == 1) | (z == 2)
    ends = (z == 0) | (z == 3)
    low = z < 2
    end = jnp.where(low, 0, 3)
    mid = jnp.where(low, 1, 2)
    other = 3 - mid
    far = 3 - end
    beside = z + 1 - 2 * lax.rem(z, 2)
    c1, c2, c3 = beside, other, far
    own_rows = blk(z, LOC)

    def remote(src, dst, s, v, dev):
        return pltpu.make_async_remote_copy(
            src_ref=src,
            dst_ref=dst,
            send_sem=ssem.at[s],
            recv_sem=rsem.at[v],
            device_id=dev,
            device_id_type=MESH,
        )

    def go(src, dst, s, v, dev, when=None):
        copy = remote(src, dst, s, v, dev)
        if when is None:
            copy.start()
        else:
            pl.when(when)(copy.start)
        pending.append((copy, when))

    def arrived(dst, v, when=None):
        copy = remote(dst, dst, 0, v, (r, z))
        if when is None:
            copy.wait_recv()
        else:
            pl.when(when)(copy.wait_recv)

    def local(src, dst):
        copy = pltpu.make_async_copy(src, dst, lsem.at[locals_.take(1)])
        copy.start()
        return copy

    def rows_at(first, n):
        return pl.ds(pl.multiple_of(first, n), n)

    small = [
        (gain_a_in, gain_a_all),
        (bias_a_in, bias_a_all),
        (gain_m_in, gain_m_all),
        (bias_m_in, bias_m_all),
        (bias_o_in, bias_o_all),
        (qkv_b_in, qkv_b_all),
    ]

    def share(ref, src, c):
        return ref.at[blk(c, src.shape[0])]

    vec_own = [local(src, share(dst, src, z)) for src, dst in small] + [local(up_b_in, up_b)]
    seg_own = local(seg_in, seg)
    x_own = local(x_in, x_all.at[own_rows])

    barrier = pltpu.get_barrier_semaphore()
    for step in range(1, Z):
        pl.semaphore_signal(
            barrier, inc=1, device_id=(r, lax.rem(z + step, Z)), device_id_type=MESH
        )
    for b in range(bits):
        pl.semaphore_signal(barrier, inc=1, device_id=(flip(r, b), z), device_id_type=MESH)
    pl.semaphore_wait(barrier, Z - 1 + bits)

    order_a = list(range(nb))
    order_b = [0, *reversed(range(1, nb))]

    def index_of(order):
        return sum(bit_of(r, b) * (1 << (nb - 1 - k)) for k, b in enumerate(order))

    idx_a, idx_b = index_of(order_a), index_of(order_b)
    cr = LOC // chunks

    up_v, qkv_v, vec_v = recvs.take(Z), recvs.take(3 * Z), recvs.take(6 * Z)
    for step in (1, 3, 2):
        t = lax.rem(z + step, Z)
        for i, (src, dst) in enumerate(small):
            go(src, share(dst, src, z), sends.take(1), vec_v + i * Z + z, (r, t))
    for step in (1, 3, 2):
        t = lax.rem(z + step, Z)
        go(
            up_w.at[blk(idx_a, cr), blk(t, 1024)],
            wup.at[rows_at(z * LOC + idx_a * cr, cr)],
            sends.take(1),
            up_v + z,
            (r, t),
        )
        for s in range(3):
            go(
                qkv_w.at[blk(idx_b, cr), rows_at(s * D + t * 256, 256)],
                wqkv.at[rows_at(z * LOC + idx_b * cr, cr), pl.ds(s * 256, 256)],
                sends.take(1),
                qkv_v + z * 3 + s,
                (r, t),
            )

    piece = LOC // SUB

    class Gather:
        def __init__(self, src, buf):
            self.src, self.buf = src, buf
            self.v = recvs.take(Z * SUB)

        def rows(self, c, k):
            return self.buf.at[rows_at(c * LOC + k * piece, piece)]

        def send(self):
            for k in range(SUB):
                for dev, when in ((mid, ends), (end, middle), (other, middle)):
                    go(
                        self.src.at[pl.ds(k * piece, piece)],
                        self.rows(z, k),
                        sends.take(1),
                        self.v + z * SUB + k,
                        (r, dev),
                        when,
                    )

        def hand(self, c, dev):
            for k in range(SUB):
                arrived(self.rows(c, k), self.v + c * SUB + k, middle)
                go(
                    self.rows(c, k),
                    self.rows(c, k),
                    sends.take(1),
                    self.v + c * SUB + k,
                    (r, dev),
                    middle,
                )

        def wait(self, c):
            for k in range(SUB):
                arrived(self.rows(c, k), self.v + c * SUB + k, ends)

    gx, gg = Gather(x_in, x_all), Gather(og_in, og_all)
    gx.send()
    own_up = local(up_w.at[:, blk(z, 1024)], wup.at[own_rows])
    own_qkv = [
        local(qkv_w.at[:, rows_at(s * D + z * 256, 256)], wqkv.at[own_rows, pl.ds(s * 256, 256)])
        for s in range(3)
    ]
    og_own = local(og_in, og_all.at[own_rows])
    w_own = [local(out_w, wout), local(down_w, wdown)]

    ag_v = recvs.take(3 * 2 * nb)

    def weight_region(kind, zz, first, n):
        ref = wup if kind == 0 else wqkv
        return ref.at[pl.ds(pl.multiple_of(zz * LOC + first * cr, cr), n * cr)]

    def weight_step(k):
        for j in range(1, Z):
            zz = lax.rem(z + j, Z)
            for kind, order, idx in ((0, order_a, idx_a), (1, order_b, idx_b)):
                b = order[nb - 1 - k]
                size = 1 << k
                first = lax.div(idx, size) * size
                go(
                    weight_region(kind, zz, first, size),
                    weight_region(kind, zz, first, size),
                    sends.take(1),
                    ag_v + ((j - 1) * 2 + kind) * nb + k,
                    (flip(r, b), z),
                )

    def weight_wait(k):
        for j in range(1, Z):
            zz = lax.rem(z + j, Z)
            for kind, idx in ((0, idx_a), (1, idx_b)):
                size = 1 << k
                first = flip(lax.div(idx, size), 0) * size
                arrived(weight_region(kind, zz, first, size), ag_v + ((j - 1) * 2 + kind) * nb + k)

    seg_own.wait()
    lane = lax.broadcasted_iota(jnp.int32, (QB, 128), 1)
    turned = lax.rem(lane, HEAD) < ROT
    ids = seg[...]
    count0 = jnp.sum((ids == 0).astype(F32), axis=1, keepdims=True)
    count1 = jnp.sum((ids <= 1).astype(F32), axis=1, keepdims=True)
    begin = jnp.where(ids == 0, 0.0, jnp.where(ids == 1, count0, count1))
    begin8 = jnp.broadcast_to(begin, (8, TOK))
    position = lax.broadcasted_iota(jnp.int32, (8, TOK), 1).astype(F32) - begin8
    turn = lax.broadcasted_iota(jnp.int32, (8, TOK), 0)
    freq = jnp.zeros((8, TOK), F32)
    for i in range(ROT // 2):
        rate = np.float32(1.0) / np.float32(10000.0) ** np.float32(i * 2.0 / ROT)
        freq = jnp.where(turn == i, float(rate), freq)
    angles = position * freq
    cosines, sines = jnp.cos(angles), jnp.sin(angles)
    for i in range(TOK // 128):
        at = slice(128 * i, 128 * i + 128)
        cosine, sine, first = cosines[:, at], sines[:, at], begin8[:, at]
        none = jnp.zeros_like(cosine)
        half = [cosine, cosine, -sine, none, none, sine, first, none]
        wide = jnp.concatenate(half + half, axis=0).T
        tab_c[at, :] = jnp.where(turned, wide, 1.0)
        tab_a[at, :] = jnp.where(turned, pltpu.roll(wide, 112, 1), 0.0)
        tab_b[at, :] = jnp.where(turned, pltpu.roll(wide, 96, 1), 0.0)
        start[at, :] = wide[:, 48:49]

    for copy in vec_own:
        copy.wait()
    x_own.wait()
    for j in range(1, Z):
        zz = lax.rem(z + j, Z)
        for i, (src, dst) in enumerate(small):
            arrived(share(dst, src, zz), vec_v + i * Z + zz)

    def flat(piece):
        return piece.astype(F32).reshape(1, piece.shape[0])

    gain_a, bias_a, gain_m, bias_m, bias_o = [flat(dst[...]) for _, dst in small[:5]]
    qkv_b = [flat(qkv_b_all[blk(s * Z + z, 256)]) for s in range(3)]
    up_shift = flat(up_b[...])

    def norm_rows(c):
        def norm(i, carry):
            rows = rows_at(c * LOC + i * 16, 16)
            v = x_all[rows, :].astype(F32)
            mean = jnp.mean(v, axis=1, keepdims=True)
            cen = v - mean
            rstd = lax.rsqrt(jnp.mean(cen * cen, axis=1, keepdims=True) + EPS)
            xhat = cen * rstd
            attn_n[rows, :] = (xhat * gain_a + bias_a).astype(BF)
            mlp_n[rows, :] = (xhat * gain_m + bias_m).astype(BF)
            mean_s[rows, :] = mean
            rstd_s[rows, :] = rstd
            return carry

        lax.fori_loop(0, LOC // 16, norm, 0, unroll=2)

    def rotate(t, rows, sign):
        return (
            t * tab_c[rows, :]
            + sign * (pltpu.roll(t, 120, 1) * tab_a[rows, :])
            + sign * (pltpu.roll(t, 8, 1) * tab_b[rows, :])
        )

    def project(c):
        rows = blk(c, LOC)
        res = nn(attn_n[rows, :], wqkv[...])
        for p in range(PAIRS):
            lanes = slice(128 * p, 128 * p + 128)
            t = res[:, lanes] + qkv_b[0][:, lanes]
            q_s[rows, lanes] = (rotate(t, rows, 1.0) * 0.125).astype(BF)
            t = res[:, 256 + 128 * p : 384 + 128 * p] + qkv_b[1][:, lanes]
            k_s[rows, lanes] = rotate(t, rows, 1.0).astype(BF)
        v_s[rows, :] = (res[:, 512:] + qkv_b[2]).astype(BF)
        h32[...] = nn(mlp_n[rows, :], wup[...])

        def act(i, carry):
            v = h32[blk(i, 16), :] + up_shift
            cdf = 0.5 + 0.5 * lax.erf(v * (0.5**0.5))
            at = rows_at(c * LOC + i * 16, 16)
            hidden[at, :] = (v * cdf).astype(BF)
            dgelu[at, :] = (
                cdf + v * jnp.exp(-0.5 * v * v) * (1.0 / math.sqrt(2.0 * math.pi))
            ).astype(BF)
            return carry

        lax.fori_loop(0, LOC // 16, act, 0)

    def twice(t):
        zero = jnp.zeros_like(t)
        return jnp.concatenate(
            [jnp.where(lane < HEAD, t, zero), jnp.where(lane >= HEAD, t, zero)], axis=0
        )

    def fold(t):
        return jnp.where(lane < HEAD, t[:QB], t[QB:])

    def window(i):
        first = pl.multiple_of(jnp.maximum(i * QB - (KB - QB), 0), QB)
        at = first + lax.broadcasted_iota(jnp.int32, (QB, KB), 1)
        row = i * QB + lax.broadcasted_iota(jnp.int32, (QB, KB), 0)
        ok = (at <= row) & (at.astype(F32) >= start[blk(i, QB), :])
        bias = jnp.where(ok, 0.0, -1e30)
        return pl.ds(first, KB), jnp.concatenate([bias, bias], axis=0)

    def attend(c):
        @pl.loop(0, LOC // QB)
        def _(j):
            i = c * (LOC // QB) + j
            keys, bias = window(i)
            rows = blk(i, QB)
            for p in range(PAIRS):
                lanes = slice(128 * p, 128 * p + 128)
                s = nt(twice(q_s[rows, lanes]), k_s[keys, lanes]) + bias
                top = jnp.max(s, axis=1, keepdims=True)
                e = jnp.exp(s - top)
                total = jnp.sum(e, axis=1, keepdims=True)
                lse[p, blk(i, 2 * QB), :] = top + jnp.log(total)
                prob = (e * (1.0 / total)).astype(BF)
                ctx[rows, lanes] = fold(nn(prob, v_s[keys, lanes])).astype(BF)

    class Scatter:
        def __init__(self, part, own, land):
            self.part, self.own, self.land = part, own, land
            self.v = recvs.take(5 * SUB)

        def slot(self, s, k):
            return self.land.at[rows_at(s * LOC + k * piece, piece)]

        def rows(self, c, k):
            return self.part.at[rows_at(c * LOC + k * piece, piece)]

        def send(self, c):
            place = jnp.clip(jnp.where(low, 3 - c, c), 0, 2)
            when = ends & (c != z)
            for k in range(SUB):
                go(
                    self.rows(c, k),
                    self.slot(place, k),
                    sends.take(1),
                    self.v + place * SUB + k,
                    (r, mid),
                    when,
                )

        def pass_on(self, came, c, dev, goes, when):
            for k in range(SUB):
                arrived(self.slot(came, k), self.v + came * SUB + k, when)

                @pl.when(when)
                def _():
                    def add(i, carry):
                        at = rows_at(c * LOC + k * piece + i * 16, 16)
                        got = rows_at(came * LOC + k * piece + i * 16, 16)
                        self.part[at, :] = self.part[at, :] + self.land[got, :]
                        return carry

                    lax.fori_loop(0, piece // 16, add, 0, unroll=2)

                go(
                    self.rows(c, k),
                    self.slot(goes, k),
                    sends.take(1),
                    self.v + goes * SUB + k,
                    (r, dev),
                    when,
                )

        def pass_far(self, when):
            self.pass_on(0, far, other, 3, when)

        def pass_other(self, when):
            self.pass_on(1, other, other, 4, when)

        def pass_end(self, when):
            self.pass_on(3, end, end, 0, when)

        def finish(self):
            for came, when in ((0, ends), (2, middle), (4, middle)):
                for k in range(SUB):
                    arrived(self.slot(came, k), self.v + came * SUB + k, when)

                @pl.when(when)
                def _():
                    def add(i, carry):
                        got = self.land[rows_at(came * LOC + i * 16, 16), :]
                        self.own[blk(i, 16), :] += got.astype(F32)
                        return carry

                    lax.fori_loop(0, LOC // 16, add, 0, unroll=2)

    s_out = Scatter(part_o, own_o, land_o)
    s_in = Scatter(part_i, own_i, land_i)

    def mix(c):
        rows = blk(c, LOC)
        res = nn(ctx[rows, :], wout[...]) + nn(hidden[rows, :], wdown[...])
        if c is z:
            own_o[...] = res + x_all[own_rows, :].astype(F32) + bias_o
        else:
            part_o[rows, :] = res.astype(BF)
            s_out.send(c)

    vsum[...] = jnp.zeros_like(vsum)
    acc[...] = jnp.zeros_like(acc)
    dk[...] = jnp.zeros_like(dk)
    dv[...] = jnp.zeros_like(dv)

    def side(c):
        rows = blk(c, LOC)
        gctx[rows, :] = nt(og_all[rows, :], wout[...]).astype(BF)
        h32[...] = nt(og_all[rows, :], wdown[...])

        def act(i, carry):
            at = rows_at(c * LOC + i * 16, 16)
            g = (h32[blk(i, 16), :] * dgelu[at, :].astype(F32)).astype(BF)
            dgelu[at, :] = g
            return carry + g.astype(F32)

        total = lax.fori_loop(0, LOC // 16, act, jnp.zeros((16, 1024), F32))
        vsum[pl.ds(7 + z, 1), :] += jnp.sum(total, axis=0, keepdims=True)

    dhid = dgelu

    def attend_back(c):
        @pl.loop(0, LOC // QB)
        def _(j):
            i = c * (LOC // QB) + j
            keys, bias = window(i)
            rows = blk(i, QB)
            for p in range(PAIRS):
                lanes = slice(128 * p, 128 * p + 128)
                q2 = twice(q_s[rows, lanes])
                kk = k_s[keys, lanes]
                g2 = twice(gctx[rows, lanes])
                s = nt(q2, kk) + bias
                prob = jnp.exp(s - lse[p, blk(i, 2 * QB), :])
                dp = nt(g2, v_s[keys, lanes])
                inner = jnp.sum(prob * dp, axis=1, keepdims=True)
                ds = (prob * (dp - inner)).astype(BF)
                dq[rows, lanes] = fold(nn(ds, kk)) * 0.125
                dk[keys, lanes] += tn(ds, q2)
                dv[keys, lanes] += tn(prob.astype(BF), g2)

    def turn_back():
        @pl.loop(0, Z)
        def _(c):
            rows = blk(c, LOC)
            for p in range(PAIRS):
                lanes = slice(128 * p, 128 * p + 128)
                dqkv[rows, lanes] = rotate(dq[rows, lanes], rows, -1.0).astype(BF)
                dqkv[rows, 256 + 128 * p : 384 + 128 * p] = rotate(dk[rows, lanes], rows, -1.0).astype(BF)
            dqkv[rows, 512:] = dv[rows, :].astype(BF)
            sums = jnp.sum(dqkv[rows, :].astype(F32), axis=0, keepdims=True)
            for s in range(3):
                vsum[4 + s : 5 + s, blk(z, 256)] += sums[:, 256 * s : 256 * s + 256]

    def inward(c):
        rows = blk(c, LOC)
        g32[...] = nt(dqkv[rows, :], wqkv[...])
        h32[...] = nt(dhid[rows, :], wup[...])

        def step(i, carry):
            at = rows_at(c * LOC + i * 16, 16)
            here = blk(i, 16)
            xhat = (x_all[at, :].astype(F32) - mean_s[at, :]) * rstd_s[at, :]
            ga, gm = g32[here, :], h32[here, :]
            for k, v in enumerate((ga * xhat, gm * xhat)):
                acc[k] += v[:8] + v[8:]
            g = ga * gain_a + gm * gain_m
            if c is z:
                own_i[here, :] = g
            else:
                part_i[at, :] = g.astype(BF)
            return carry

        lax.fori_loop(0, LOC // 16, step, 0)

    def through(sums, weight):
        parts, rest = [], sums
        for _ in range(3):
            part = rest.astype(BF).astype(F32)
            parts.append(part)
            rest = rest - part
        parts.append(jnp.zeros((13, sums.shape[1]), F32))
        return jnp.sum(nt(jnp.concatenate(parts, axis=0).astype(BF), weight[...]), axis=0, keepdims=True)

    cd = FF // Z // chunks

    def weights_down():
        g_od[:, cd:, :] = tn(ctx[...], og_all[...]).reshape(chunks, cr, D).astype(BF)

        @pl.loop(0, Z)
        def _(i):
            got = tn(hidden[:, blk(i, 256)], og_all[...])
            g_od[blk(i, 256 // cd), :cd, :] = got.reshape(256 // cd, cd, D).astype(BF)

    def weights_up():
        @pl.loop(0, Z)
        def _(i):
            g_up[i] = tn(mlp_n[:, blk(i, 256)], dhid[...]).astype(BF)

    def weights_qkv():
        @pl.loop(0, Z)
        def _(c):
            g_qkv[c] = tn(attn_n[:, blk(c, 256)], dqkv[...]).astype(BF)

    class Stream:
        def __init__(self, order, grad, temp, final, across=None):
            self.order, self.idx = order, index_of(order)
            self.grad, self.temp, self.final, self.across = grad, temp, final, across
            self.v, self.g = recvs.take(bits), recvs.take(nb)
            self.zv = recvs.take(Z) if across else None
            self.first, self.size, self.off = 0, chunks, 0

        def halve(self, k):
            if k < nb:
                self.size //= 2
                b = self.order[k]
                keep = self.first + bit_of(r, b) * self.size
                give = self.first + (1 - bit_of(r, b)) * self.size
            else:
                b, keep, give = k, self.first, self.first
            self.keep = keep
            self.at = len(pending)
            go(
                self.grad(give, self.size),
                self.temp(self.off, self.size),
                sends.take(1),
                self.v + k,
                (flip(r, b), z),
            )

        def add(self, k):
            got = self.temp(self.off, self.size)
            arrived(got, self.v + k)
            keep = self.grad(self.keep, self.size)
            if k >= nb:
                pending[self.at][0].wait_send()
                pending[self.at] = None
            n = keep.shape[1] // 16

            def step(j, carry):
                i, at = lax.div(j, n), blk(lax.rem(j, n), 16)
                keep[i, at, :] = keep[i, at, :] + got[i, at, :]
                return carry

            lax.fori_loop(0, keep.shape[0] * n, step, 0, unroll=4)
            self.off += self.size
            self.first = self.keep

        def place(self):
            if self.across is None:
                self.put = local(self.grad(self.idx, 1), self.final(self.idx, 1))
                return
            src, dst = self.across
            for step in (2, 1, 3):
                t = lax.rem(z + step, Z)
                go(src(t, self.idx), dst(z, self.idx), sends.take(1), self.zv + z, (r, t))
            self.put = local(src(z, self.idx), dst(z, self.idx))

        def placed(self):
            if self.across is not None:
                for step in (1, 3, 2):
                    t = lax.rem(z + step, Z)
                    arrived(self.across[1](t, self.idx), self.zv + t)
            self.put.wait()

        def gather(self, k):
            size = 1 << k
            first = lax.div(self.idx, size) * size
            go(
                self.final(first, size),
                self.final(first, size),
                sends.take(1),
                self.g + k,
                (flip(r, self.order[nb - 1 - k]), z),
            )

        def gathered(self, k):
            size = 1 << k
            first = flip(lax.div(self.idx, size), 0) * size
            arrived(self.final(first, size), self.g + k)

    def chunk_rows(ref, lanes):
        return lambda first, n: ref.at[pl.ds(first, n), :, lanes]

    def deep_rows(ref, lanes):
        return lambda first, n: ref.at[:, pl.ds(pl.multiple_of(first * cr, cr), n * cr), lanes]

    def deep_block(ref, lanes):
        return lambda t, idx: ref.at[t, rows_at(idx * cr, cr), lanes]

    def pair(grad, temp, final, width, across):
        made = []
        for order, lanes in ((order_a, pl.ds(0, width)), (order_b, pl.ds(width, width))):
            if across:
                refs = [deep_rows(ref, lanes) for ref in (grad, temp, final)]
                both = (deep_block(grad, lanes), deep_block(final, lanes))
                made.append(Stream(order, *refs, both))
            else:
                made.append(Stream(order, *[chunk_rows(ref, lanes) for ref in (grad, temp, final)]))
        return made

    class Group:
        def __init__(self, streams):
            self.streams, self.at = streams, 0

        def all(self, name, *args):
            for s in self.streams:
                getattr(s, name)(*args)

        def go_on(self, times=1):
            for _ in range(times):
                n = self.at
                if 0 < n <= bits:
                    self.all("add", n - 1)
                if n < bits:
                    self.all("halve", n)
                elif n == bits:
                    self.all("place")
                elif n == bits + 1:
                    self.all("placed")
                else:
                    self.all("gathered", n - bits - 2)
                if bits + 1 <= n < bits + 1 + nb:
                    self.all("gather", n - bits - 1)
                self.at += 1

    down = Group(pair(g_od, t_od, f_od, 512, False))
    up = Group(pair(g_up, t_up, f_up, 512, True))
    qkv = Group(pair(g_qkv, t_qkv, f_qkv, 384, True))
    total_steps = bits + 2 + nb

    vec_steps = [(0, b) for b in range(bits)] + [(1, b) for b in range(2)]
    vec_v2 = recvs.take(len(vec_steps))
    vec_at = [0]

    def vec_on():
        n = vec_at[0]
        if n > len(vec_steps):
            return
        if n > 0:
            arrived(vrecv.at[n - 1], vec_v2 + n - 1)
            pending[vec_at[1]][0].wait_send()
            pending[vec_at[1]] = None
            vsum[...] = vsum[...] + vrecv[n - 1]
        if n < len(vec_steps):
            axis, b = vec_steps[n]
            dev = (flip(r, b), z) if axis == 0 else (r, flip(z, b))
            vec_at[1:] = [len(pending)]
            go(vsum, vrecv.at[n], sends.take(1), vec_v2 + n, dev)
        vec_at[0] += 1

    norm_rows(z)
    for j in range(1, Z):
        zz = lax.rem(z + j, Z)
        arrived(weight_region(0, zz, idx_a, 1), up_v + zz)
        for s in range(3):
            arrived(
                wqkv.at[rows_at(zz * LOC + idx_b * cr, cr), pl.ds(s * 256, 256)],
                qkv_v + zz * 3 + s,
            )
    for k in range(nb):
        weight_step(k)
        if k == 1:
            gx.hand(c1, other)
            gx.hand(c2, end)
        if k == nb - 1:
            gx.wait(c1)
            norm_rows(c1)
        weight_wait(k)
    own_up.wait()
    for copy in own_qkv:
        copy.wait()
    gx.hand(c3, end)
    project(z)
    project(c1)
    gx.wait(c2)
    norm_rows(c2)
    project(c2)
    gx.wait(c3)
    gg.send()
    norm_rows(c3)
    project(c3)
    for copy in w_own:
        copy.wait()
    attend(c3)
    mix(c3)
    attend(c2)
    mix(c2)
    gg.hand(c1, other)
    gg.hand(c2, end)
    attend(c1)
    mix(c1)
    attend(z)
    mix(z)
    og_own.wait()
    side(z)
    gg.wait(c1)
    side(c1)
    gg.hand(c3, end)
    attend_back(z)
    attend_back(c1)
    s_out.pass_far(middle)
    gg.wait(c2)
    side(c2)
    attend_back(c2)
    s_out.pass_other(middle)
    gg.wait(c3)
    weights_down()
    down.go_on()
    side(c3)
    weights_up()
    down.go_on()
    up.go_on()
    attend_back(c3)
    up.go_on()
    s_out.pass_end(middle)
    turn_back()
    weights_qkv()
    qkv.go_on()
    down.go_on()
    inward(c3)
    s_in.send(c3)
    qkv.go_on()
    inward(c2)
    down.go_on(2)
    up.go_on()
    inward(c1)
    s_in.send(c2)
    inward(z)
    up.go_on()
    down.go_on()
    qkv.go_on()

    def add_og(i, carry):
        return carry + og_all[rows_at(z * LOC + i * 16, 16), :].astype(F32)

    vsum[11:12, :] = jnp.sum(
        lax.fori_loop(0, LOC // 16, add_og, jnp.zeros((16, 1024), F32)), axis=0, keepdims=True
    )
    sums = jnp.concatenate([vsum[4 + s : 5 + s, blk(z, 256)] for s in range(3)], axis=1)
    vsum[0:1, :] = jnp.sum(acc[0], axis=0, keepdims=True)
    vsum[1:2, :] = through(sums, wqkv)
    vsum[2:3, :] = jnp.sum(acc[1], axis=0, keepdims=True)
    vsum[3:4, :] = through(vsum[pl.ds(7 + z, 1), :], wup)
    vec_on()
    s_in.pass_far(middle)
    s_out.finish()
    part_o[own_rows, :] = own_o[...].astype(BF)
    copies = [local(part_o.at[own_rows], outputs)]
    qkv.go_on()
    up.go_on()
    vec_on()
    s_in.send(c1)
    down.go_on()
    s_in.pass_other(middle)
    vec_on()
    up.go_on()
    qkv.go_on()
    vec_on()
    s_in.pass_end(middle)
    while qkv.at < total_steps - 1:
        qkv.go_on()
        vec_on()
        if up.at < total_steps:
            up.go_on()
        if down.at < total_steps:
            down.go_on()
    vec_on()
    s_in.finish()

    def finish(i, carry):
        rows = blk(i, 16)
        at = rows_at(z * LOC + i * 16, 16)
        rstd = rstd_s[at, :]
        xhat = (x_all[at, :].astype(F32) - mean_s[at, :]) * rstd
        g = own_i[rows, :]
        m1 = jnp.mean(g, axis=1, keepdims=True)
        m2 = jnp.mean(g * xhat, axis=1, keepdims=True)
        res = rstd * (g - m1 - xhat * m2)
        part_i[at, :] = (og_all[at, :].astype(F32) + res).astype(BF)
        return carry

    lax.fori_loop(0, LOC // 16, finish, 0, unroll=2)
    copies.append(local(part_i.at[own_rows], in_grad))
    while vec_at[0] <= len(vec_steps):
        vec_on()
    vec_out[...] = vsum[...]
    for group in (qkv, up, down):
        while group.at < total_steps:
            group.go_on()
    for copy in copies:
        copy.wait()
    for copy, when in [p for p in pending if p is not None]:
        if when is None:
            copy.wait_send()
        else:
            pl.when(when)(copy.wait_send)


def tail(outs_in, in_in, f_qkv, f_up, f_od, vec, *results):
    z = lax.axis_index("shard")
    outs, ingrad, gga, gba, ggm, gbm, gqkv, gqkvb, gout, gup, gupb, gdown, goutb = results
    outs[...] = outs_in[...]
    ingrad[...] = in_in[...]
    for t in range(Z):
        gup[:, 1024 * t : 1024 * t + 1024] = f_up[t].astype(F32)
        for s in range(3):
            first = D * s + 256 * t
            gqkv[:, first : first + 256] = f_qkv[t, :, 256 * s : 256 * s + 256].astype(F32)
    n, m = gdown.shape[0] // f_od.shape[0], gout.shape[0] // f_od.shape[0]
    for i in range(f_od.shape[0]):
        gdown[n * i : n * i + n, :] = f_od[i, :n].astype(F32)
        gout[m * i : m * i + m, :] = f_od[i, n:].astype(F32)

    @pl.when(pl.program_id(0) == 0)
    def _():
        for k, ref in ((0, gga), (1, gba), (2, ggm), (3, gbm), (11, goutb)):
            ref[...] = vec[k : k + 1, blk(z, 256)].reshape(256)
        for i in range(3):
            g = 3 * z + i
            piece = vec[pl.ds(4 + lax.div(g, Z), 1), blk(lax.rem(g, Z), 256)]
            gqkvb[256 * i : 256 * i + 256] = piece.reshape(256)
        gupb[...] = vec[pl.ds(7 + z, 1), :].reshape(1024)


def shards(
    replicas,
    inputs,
    out_grad,
    segment_ids,
    ln_gain_attn,
    ln_bias_attn,
    ln_gain_mlp,
    ln_bias_mlp,
    qkv_weight,
    qkv_bias,
    out_weight,
    up_weight,
    up_bias,
    down_weight,
    output_bias,
):
    bits = int(math.log2(replicas))
    chunks = 1 << min(bits, 4)
    vm = pl.BlockSpec(memory_space=pltpu.VMEM)
    hbm = pl.BlockSpec(memory_space=pl.ANY)

    def v(*shape, dtype=BF):
        return pltpu.VMEM(shape, dtype)

    scratch = dict(
        x_all=v(TOK, D),
        og_all=v(TOK, D),
        gain_a_all=v(D),
        bias_a_all=v(D),
        gain_m_all=v(D),
        bias_m_all=v(D),
        bias_o_all=v(D),
        qkv_b_all=v(3 * D),
        up_b=v(1024),
        seg=pltpu.VMEM((1, TOK), jnp.int32),
        tab_c=v(TOK, 128, dtype=F32),
        tab_a=v(TOK, 128, dtype=F32),
        tab_b=v(TOK, 128, dtype=F32),
        start=v(TOK, 1, dtype=F32),
        wqkv=v(D, 768),
        wup=v(D, 1024),
        wout=v(256, D),
        wdown=v(1024, D),
        attn_n=v(TOK, D),
        mlp_n=v(TOK, D),
        mean_s=v(TOK, 1, dtype=F32),
        rstd_s=v(TOK, 1, dtype=F32),
        q_s=v(TOK, 256),
        k_s=v(TOK, 256),
        v_s=v(TOK, 256),
        ctx=v(TOK, 256),
        lse=v(PAIRS, 2 * TOK, 1, dtype=F32),
        h32=v(LOC, 1024, dtype=F32),
        g32=v(LOC, 1024, dtype=F32),
        acc=v(2, 8, 1024, dtype=F32),
        hidden=v(TOK, 1024),
        dgelu=v(TOK, 1024),
        part_o=v(TOK, D),
        part_i=v(TOK, D),
        own_o=v(LOC, D, dtype=F32),
        own_i=v(LOC, D, dtype=F32),
        land_o=v(5 * LOC, D),
        land_i=v(5 * LOC, D),
        gctx=v(TOK, 256),
        dq=v(TOK, 256, dtype=F32),
        dk=v(TOK, 256, dtype=F32),
        dv=v(TOK, 256, dtype=F32),
        dqkv=v(TOK, 768),
        g_qkv=v(Z, 256, 768),
        g_up=v(Z, 256, 1024),
        g_od=v(chunks, 1280 // chunks, D),
        t_qkv=v(Z, 256, 768),
        t_up=v(Z, 256, 1024),
        t_od=v(chunks, 1280 // chunks, D),
        vsum=v(16, 1024, dtype=F32),
        vrecv=v(bits + 2, 16, 1024, dtype=F32),
        ssem=pltpu.SemaphoreType.DMA((NSEM,)),
        rsem=pltpu.SemaphoreType.DMA((NSEM,)),
        lsem=pltpu.SemaphoreType.DMA((32,)),
    )
    names = list(scratch)

    def body(*refs):
        layer(replicas, *refs[:20], **dict(zip(names, refs[20:])))

    res = pl.pallas_call(
        body,
        out_shape=[
            jax.ShapeDtypeStruct((LOC, D), BF),
            jax.ShapeDtypeStruct((LOC, D), BF),
            jax.ShapeDtypeStruct((Z, 256, 768), BF),
            jax.ShapeDtypeStruct((Z, 256, 1024), BF),
            jax.ShapeDtypeStruct((chunks, 1280 // chunks, D), BF),
            jax.ShapeDtypeStruct((16, 1024), F32),
        ],
        in_specs=[hbm] * 14,
        out_specs=[hbm, hbm, hbm, hbm, hbm, vm],
        scratch_shapes=list(scratch.values()),
        compiler_params=pltpu.CompilerParams(
            collective_id=0,
            has_side_effects=True,
            vmem_limit_bytes=61 * 2**20,
        ),
    )(
        inputs.reshape(LOC, D),
        out_grad.reshape(LOC, D),
        qkv_weight,
        up_weight,
        out_weight,
        down_weight,
        ln_gain_attn,
        ln_bias_attn,
        ln_gain_mlp,
        ln_bias_mlp,
        output_bias,
        qkv_bias,
        up_bias,
        segment_ids,
    )
    steps = chunks // 2
    n = LOC // steps
    row = pl.BlockSpec((n, D), lambda i: (i, 0))
    tall = pl.BlockSpec((1024 // steps, D), lambda i: (i, 0))

    def fixed(w):
        return pl.BlockSpec((w,), lambda i: (0,))

    small, wide = [fixed(256)], [fixed(768)]
    final = pl.pallas_call(
        tail,
        grid=(steps,),
        in_specs=[
            row,
            row,
            pl.BlockSpec((Z, n, 768), lambda i: (0, i, 0)),
            pl.BlockSpec((Z, n, 1024), lambda i: (0, i, 0)),
            pl.BlockSpec((2, 1280 // chunks, D), lambda i: (i, 0, 0)),
            pl.BlockSpec((16, 1024), lambda i: (0, 0)),
        ],
        out_specs=[row, row]
        + small * 4
        + [pl.BlockSpec((n, 3 * D), lambda i: (i, 0))]
        + wide
        + [row, pl.BlockSpec((n, FF), lambda i: (i, 0)), fixed(1024), tall]
        + small,
        out_shape=[jax.ShapeDtypeStruct((LOC, D), BF)] * 2
        + [jax.ShapeDtypeStruct((256,), F32)] * 4
        + [
            jax.ShapeDtypeStruct((256, 3 * D), F32),
            jax.ShapeDtypeStruct((768,), F32),
            jax.ShapeDtypeStruct((256, D), F32),
            jax.ShapeDtypeStruct((256, FF), F32),
            jax.ShapeDtypeStruct((1024,), F32),
            jax.ShapeDtypeStruct((1024, D), F32),
            jax.ShapeDtypeStruct((256,), F32),
        ],
    )(*res)
    return tuple(a.reshape(1, LOC, D) for a in final[:2]) + tuple(final[2:])


def solution(mesh):
    seq = P("replica", "shard", None)
    row = P("shard", None)
    one = P("shard")
    return jax.shard_map(
        partial(shards, mesh.shape["replica"]),
        mesh=mesh,
        in_specs=(seq, seq, P("replica", None), one, one, one, one, row, one, row, row, one, row, one),
        out_specs=(seq, seq, one, one, one, one, row, one, row, row, one, row, one),
        check_vma=False,
    )
```

```python
import math
from functools import partial

import jax
import jax.numpy as jnp
import numpy as np
from jax import lax
from jax.experimental import pallas as pl
from jax.experimental.pallas import tpu as pltpu
from jax.sharding import PartitionSpec as P

D = 1024
FF = 4096
HEADS = 16
HEAD = 64
ROT = 16
Z = 4
LOC = 256
TOK = 1024
PAIRS = 2
QB = 128
KB = 640
EPS = 1e-05
BF = jnp.bfloat16
F32 = jnp.float32
MESH = pl.DeviceIdType.MESH
NSEM = 256
SUB = 2


def bit_of(value, place):
    return lax.rem(lax.div(value, 1 << place), 2)


def flip(value, place):
    return value + (1 - 2 * bit_of(value, place)) * (1 << place)


def nn(a, b):
    return jnp.dot(a, b, preferred_element_type=F32)


def nt(a, b):
    return lax.dot_general(a, b, (((1,), (1,)), ((), ())), preferred_element_type=F32)


def tn(a, b):
    return lax.dot_general(a, b, (((0,), (0,)), ((), ())), preferred_element_type=F32)


def blk(i, n):
    return pl.ds(pl.multiple_of(i * n, n), n)


class Count:
    def __init__(self):
        self.used = 0

    def take(self, n):
        first = self.used
        self.used += n
        assert self.used <= NSEM
        return first


def layer(
    replicas,
    x_in,
    og_in,
    qkv_w,
    up_w,
    out_w,
    down_w,
    gain_a_in,
    bias_a_in,
    gain_m_in,
    bias_m_in,
    bias_o_in,
    qkv_b_in,
    up_b_in,
    seg_in,
    outputs,
    in_grad,
    f_qkv,
    f_up,
    f_od,
    vec_out,
    x_all,
    og_all,
    gain_a_all,
    bias_a_all,
    gain_m_all,
    bias_m_all,
    bias_o_all,
    qkv_b_all,
    up_b,
    seg,
    tab_c,
    tab_a,
    tab_b,
    start,
    wqkv,
    wup,
    wout,
    wdown,
    attn_n,
    mlp_n,
    mean_s,
    rstd_s,
    q_s,
    k_s,
    v_s,
    ctx,
    lse,
    h32,
    g32,
    acc,
    hidden,
    dgelu,
    part_o,
    part_i,
    own_o,
    own_i,
    land_o,
    land_i,
    gctx,
    dq,
    dk,
    dv,
    dqkv,
    g_qkv,
    g_up,
    g_od,
    t_qkv,
    t_up,
    t_od,
    vsum,
    vrecv,
    ssem,
    rsem,
    lsem,
):
    r = lax.axis_index("replica")
    z = lax.axis_index("shard")
    bits = int(math.log2(replicas))
    nb = min(bits, 4)
    chunks = 1 << nb
    sends, recvs, locals_ = Count(), Count(), Count()
    pending = []

    middle = (z == 1) | (z == 2)
    ends = (z == 0) | (z == 3)
    low = z < 2
    end = jnp.where(low, 0, 3)
    mid = jnp.where(low, 1, 2)
    other = 3 - mid
    far = 3 - end
    beside = z + 1 - 2 * lax.rem(z, 2)
    c1, c2, c3 = beside, other, far
    own_rows = blk(z, LOC)

    def remote(src, dst, s, v, dev):
        return pltpu.make_async_remote_copy(
            src_ref=src,
            dst_ref=dst,
            send_sem=ssem.at[s],
            recv_sem=rsem.at[v],
            device_id=dev,
            device_id_type=MESH,
        )

    def go(src, dst, s, v, dev, when=None):
        copy = remote(src, dst, s, v, dev)
        if when is None:
            copy.start()
        else:
            pl.when(when)(copy.start)
        pending.append((copy, when))

    def arrived(dst, v, when=None):
        copy = remote(dst, dst, 0, v, (r, z))
        if when is None:
            copy.wait_recv()
        else:
            pl.when(when)(copy.wait_recv)

    def local(src, dst):
        copy = pltpu.make_async_copy(src, dst, lsem.at[locals_.take(1)])
        copy.start()
        return copy

    def rows_at(first, n):
        return pl.ds(pl.multiple_of(first, n), n)

    small = [
        (gain_a_in, gain_a_all),
        (bias_a_in, bias_a_all),
        (gain_m_in, gain_m_all),
        (bias_m_in, bias_m_all),
        (bias_o_in, bias_o_all),
        (qkv_b_in, qkv_b_all),
    ]

    def share(ref, src, c):
        return ref.at[blk(c, src.shape[0])]

    vec_own = [local(src, share(dst, src, z)) for src, dst in small] + [local(up_b_in, up_b)]
    seg_own = local(seg_in, seg)
    x_own = local(x_in, x_all.at[own_rows])

    barrier = pltpu.get_barrier_semaphore()
    for step in range(1, Z):
        pl.semaphore_signal(
            barrier, inc=1, device_id=(r, lax.rem(z + step, Z)), device_id_type=MESH
        )
    for b in range(bits):
        pl.semaphore_signal(barrier, inc=1, device_id=(flip(r, b), z), device_id_type=MESH)
    pl.semaphore_wait(barrier, Z - 1 + bits)

    order_a = list(range(nb))
    order_b = [0, *reversed(range(1, nb))]

    def index_of(order):
        return sum(bit_of(r, b) * (1 << (nb - 1 - k)) for k, b in enumerate(order))

    idx_a, idx_b = index_of(order_a), index_of(order_b)
    cr = LOC // chunks

    up_v, qkv_v, vec_v = recvs.take(Z), recvs.take(3 * Z), recvs.take(6 * Z)
    for step in (1, 3, 2):
        t = lax.rem(z + step, Z)
        for i, (src, dst) in enumerate(small):
            go(src, share(dst, src, z), sends.take(1), vec_v + i * Z + z, (r, t))
    for step in (1, 3, 2):
        t = lax.rem(z + step, Z)
        go(
            up_w.at[blk(idx_a, cr), blk(t, 1024)],
            wup.at[rows_at(z * LOC + idx_a * cr, cr)],
            sends.take(1),
            up_v + z,
            (r, t),
        )
        for s in range(3):
            go(
                qkv_w.at[blk(idx_b, cr), rows_at(s * D + t * 256, 256)],
                wqkv.at[rows_at(z * LOC + idx_b * cr, cr), pl.ds(s * 256, 256)],
                sends.take(1),
                qkv_v + z * 3 + s,
                (r, t),
            )

    piece = LOC // SUB

    class Gather:
        def __init__(self, src, buf):
            self.src, self.buf = src, buf
            self.v = recvs.take(Z * SUB)

        def rows(self, c, k):
            return self.buf.at[rows_at(c * LOC + k * piece, piece)]

        def send(self, ways=(0, 1, 2)):
            every = ((mid, ends), (end, middle), (other, middle))
            for k in range(SUB):
                for dev, when in [every[w] for w in ways]:
                    go(
                        self.src.at[pl.ds(k * piece, piece)],
                        self.rows(z, k),
                        sends.take(1),
                        self.v + z * SUB + k,
                        (r, dev),
                        when,
                    )

        def hand(self, c, dev):
            for k in range(SUB):
                arrived(self.rows(c, k), self.v + c * SUB + k, middle)
                go(
                    self.rows(c, k),
                    self.rows(c, k),
                    sends.take(1),
                    self.v + c * SUB + k,
                    (r, dev),
                    middle,
                )

        def wait(self, c):
            for k in range(SUB):
                arrived(self.rows(c, k), self.v + c * SUB + k, ends)

    gx, gg = Gather(x_in, x_all), Gather(og_in, og_all)
    gx.send()
    own_up = local(up_w.at[:, blk(z, 1024)], wup.at[own_rows])
    own_qkv = [
        local(qkv_w.at[:, rows_at(s * D + z * 256, 256)], wqkv.at[own_rows, pl.ds(s * 256, 256)])
        for s in range(3)
    ]
    og_own = local(og_in, og_all.at[own_rows])
    w_own = [local(out_w, wout), local(down_w, wdown)]

    ag_v = recvs.take(3 * 2 * nb)

    def weight_region(kind, zz, first, n):
        ref = wup if kind == 0 else wqkv
        return ref.at[pl.ds(pl.multiple_of(zz * LOC + first * cr, cr), n * cr)]

    def weight_step(k):
        for j in range(1, Z):
            zz = lax.rem(z + j, Z)
            for kind, order, idx in ((0, order_a, idx_a), (1, order_b, idx_b)):
                b = order[nb - 1 - k]
                size = 1 << k
                first = lax.div(idx, size) * size
                go(
                    weight_region(kind, zz, first, size),
                    weight_region(kind, zz, first, size),
                    sends.take(1),
                    ag_v + ((j - 1) * 2 + kind) * nb + k,
                    (flip(r, b), z),
                )

    def weight_wait(k):
        for j in range(1, Z):
            zz = lax.rem(z + j, Z)
            for kind, idx in ((0, idx_a), (1, idx_b)):
                size = 1 << k
                first = flip(lax.div(idx, size), 0) * size
                arrived(weight_region(kind, zz, first, size), ag_v + ((j - 1) * 2 + kind) * nb + k)

    seg_own.wait()
    lane = lax.broadcasted_iota(jnp.int32, (QB, 128), 1)
    turned = lax.rem(lane, HEAD) < ROT
    ids = seg[...]
    count0 = jnp.sum((ids == 0).astype(F32), axis=1, keepdims=True)
    count1 = jnp.sum((ids <= 1).astype(F32), axis=1, keepdims=True)
    begin = jnp.where(ids == 0, 0.0, jnp.where(ids == 1, count0, count1))
    begin8 = jnp.broadcast_to(begin, (8, TOK))
    position = lax.broadcasted_iota(jnp.int32, (8, TOK), 1).astype(F32) - begin8
    turn = lax.broadcasted_iota(jnp.int32, (8, TOK), 0)
    freq = jnp.zeros((8, TOK), F32)
    for i in range(ROT // 2):
        rate = np.float32(1.0) / np.float32(10000.0) ** np.float32(i * 2.0 / ROT)
        freq = jnp.where(turn == i, float(rate), freq)
    angles = position * freq
    cosines, sines = jnp.cos(angles), jnp.sin(angles)
    for i in range(TOK // 128):
        at = slice(128 * i, 128 * i + 128)
        cosine, sine, first = cosines[:, at], sines[:, at], begin8[:, at]
        none = jnp.zeros_like(cosine)
        half = [cosine, cosine, -sine, none, none, sine, first, none]
        wide = jnp.concatenate(half + half, axis=0).T
        tab_c[at, :] = jnp.where(turned, wide, 1.0)
        tab_a[at, :] = jnp.where(turned, pltpu.roll(wide, 112, 1), 0.0)
        tab_b[at, :] = jnp.where(turned, pltpu.roll(wide, 96, 1), 0.0)
        start[at, :] = wide[:, 48:49]

    for copy in vec_own:
        copy.wait()
    x_own.wait()
    for j in range(1, Z):
        zz = lax.rem(z + j, Z)
        for i, (src, dst) in enumerate(small):
            arrived(share(dst, src, zz), vec_v + i * Z + zz)

    def flat(piece):
        return piece.astype(F32).reshape(1, piece.shape[0])

    gain_a, bias_a, gain_m, bias_m, bias_o = [flat(dst[...]) for _, dst in small[:5]]
    qkv_b = [flat(qkv_b_all[blk(s * Z + z, 256)]) for s in range(3)]
    up_shift = flat(up_b[...])

    def norm_rows(c):
        def norm(i, carry):
            rows = rows_at(c * LOC + i * 16, 16)
            v = x_all[rows, :].astype(F32)
            mean = jnp.mean(v, axis=1, keepdims=True)
            cen = v - mean
            rstd = lax.rsqrt(jnp.mean(cen * cen, axis=1, keepdims=True) + EPS)
            xhat = cen * rstd
            attn_n[rows, :] = (xhat * gain_a + bias_a).astype(BF)
            mlp_n[rows, :] = (xhat * gain_m + bias_m).astype(BF)
            mean_s[rows, :] = mean
            rstd_s[rows, :] = rstd
            return carry

        lax.fori_loop(0, LOC // 16, norm, 0, unroll=2)

    def rotate(t, rows, sign):
        return (
            t * tab_c[rows, :]
            + sign * (pltpu.roll(t, 120, 1) * tab_a[rows, :])
            + sign * (pltpu.roll(t, 8, 1) * tab_b[rows, :])
        )

    def project(c):
        rows = blk(c, LOC)
        res = nn(attn_n[rows, :], wqkv[...])
        for p in range(PAIRS):
            lanes = slice(128 * p, 128 * p + 128)
            t = res[:, lanes] + qkv_b[0][:, lanes]
            q_s[rows, lanes] = (rotate(t, rows, 1.0) * 0.125).astype(BF)
            t = res[:, 256 + 128 * p : 384 + 128 * p] + qkv_b[1][:, lanes]
            k_s[rows, lanes] = rotate(t, rows, 1.0).astype(BF)
        v_s[rows, :] = (res[:, 512:] + qkv_b[2]).astype(BF)
        h32[...] = nn(mlp_n[rows, :], wup[...])

        def act(i, carry):
            v = h32[blk(i, 16), :] + up_shift
            cdf = 0.5 + 0.5 * lax.erf(v * (0.5**0.5))
            at = rows_at(c * LOC + i * 16, 16)
            hidden[at, :] = (v * cdf).astype(BF)
            dgelu[at, :] = (
                cdf + v * jnp.exp(-0.5 * v * v) * (1.0 / math.sqrt(2.0 * math.pi))
            ).astype(BF)
            return carry

        lax.fori_loop(0, LOC // 16, act, 0)

    def twice(t):
        zero = jnp.zeros_like(t)
        return jnp.concatenate(
            [jnp.where(lane < HEAD, t, zero), jnp.where(lane >= HEAD, t, zero)], axis=0
        )

    def fold(t):
        return jnp.where(lane < HEAD, t[:QB], t[QB:])

    def window(i):
        first = pl.multiple_of(jnp.maximum(i * QB - (KB - QB), 0), QB)
        at = first + lax.broadcasted_iota(jnp.int32, (QB, KB), 1)
        row = i * QB + lax.broadcasted_iota(jnp.int32, (QB, KB), 0)
        ok = (at <= row) & (at.astype(F32) >= start[blk(i, QB), :])
        bias = jnp.where(ok, 0.0, -1e30)
        return pl.ds(first, KB), jnp.concatenate([bias, bias], axis=0)

    def attend(c):
        @pl.loop(0, LOC // QB)
        def _(j):
            i = c * (LOC // QB) + j
            keys, bias = window(i)
            rows = blk(i, QB)
            for p in range(PAIRS):
                lanes = slice(128 * p, 128 * p + 128)
                s = nt(twice(q_s[rows, lanes]), k_s[keys, lanes]) + bias
                top = jnp.max(s, axis=1, keepdims=True)
                e = jnp.exp(s - top)
                total = jnp.sum(e, axis=1, keepdims=True)
                lse[p, blk(i, 2 * QB), :] = top + jnp.log(total)
                prob = (e * (1.0 / total)).astype(BF)
                ctx[rows, lanes] = fold(nn(prob, v_s[keys, lanes])).astype(BF)

    class Scatter:
        def __init__(self, part, own, land):
            self.part, self.own, self.land = part, own, land
            self.v = recvs.take(5 * SUB)

        def slot(self, s, k):
            return self.land.at[rows_at(s * LOC + k * piece, piece)]

        def rows(self, c, k):
            return self.part.at[rows_at(c * LOC + k * piece, piece)]

        def send(self, c):
            place = jnp.clip(jnp.where(low, 3 - c, c), 0, 2)
            when = ends & (c != z)
            for k in range(SUB):
                go(
                    self.rows(c, k),
                    self.slot(place, k),
                    sends.take(1),
                    self.v + place * SUB + k,
                    (r, mid),
                    when,
                )

        def pass_on(self, came, c, dev, goes, when):
            for k in range(SUB):
                arrived(self.slot(came, k), self.v + came * SUB + k, when)

                @pl.when(when)
                def _():
                    def add(i, carry):
                        at = rows_at(c * LOC + k * piece + i * 16, 16)
                        got = rows_at(came * LOC + k * piece + i * 16, 16)
                        self.part[at, :] = self.part[at, :] + self.land[got, :]
                        return carry

                    lax.fori_loop(0, piece // 16, add, 0, unroll=2)

                go(
                    self.rows(c, k),
                    self.slot(goes, k),
                    sends.take(1),
                    self.v + goes * SUB + k,
                    (r, dev),
                    when,
                )

        def pass_far(self, when):
            self.pass_on(0, far, other, 3, when)

        def pass_other(self, when):
            self.pass_on(1, other, other, 4, when)

        def pass_end(self, when):
            self.pass_on(3, end, end, 0, when)

        def finish(self):
            for came, when in ((0, ends), (2, middle), (4, middle)):
                for k in range(SUB):
                    arrived(self.slot(came, k), self.v + came * SUB + k, when)

                @pl.when(when)
                def _():
                    def add(i, carry):
                        got = self.land[rows_at(came * LOC + i * 16, 16), :]
                        self.own[blk(i, 16), :] += got.astype(F32)
                        return carry

                    lax.fori_loop(0, LOC // 16, add, 0, unroll=2)

    s_out = Scatter(part_o, own_o, land_o)
    s_in = Scatter(part_i, own_i, land_i)

    def mix(c):
        rows = blk(c, LOC)
        res = nn(ctx[rows, :], wout[...]) + nn(hidden[rows, :], wdown[...])
        if c is z:
            own_o[...] = res + x_all[own_rows, :].astype(F32) + bias_o
        else:
            part_o[rows, :] = res.astype(BF)
            s_out.send(c)

    vsum[...] = jnp.zeros_like(vsum)
    acc[...] = jnp.zeros_like(acc)
    dk[...] = jnp.zeros_like(dk)
    dv[...] = jnp.zeros_like(dv)

    def side(c):
        rows = blk(c, LOC)
        gctx[rows, :] = nt(og_all[rows, :], wout[...]).astype(BF)
        h32[...] = nt(og_all[rows, :], wdown[...])

        def act(i, carry):
            at = rows_at(c * LOC + i * 16, 16)
            g = (h32[blk(i, 16), :] * dgelu[at, :].astype(F32)).astype(BF)
            dgelu[at, :] = g
            return carry + g.astype(F32)

        total = lax.fori_loop(0, LOC // 16, act, jnp.zeros((16, 1024), F32))
        vsum[pl.ds(7 + z, 1), :] += jnp.sum(total, axis=0, keepdims=True)

    dhid = dgelu

    def attend_back(c):
        @pl.loop(0, LOC // QB)
        def _(j):
            i = c * (LOC // QB) + j
            keys, bias = window(i)
            rows = blk(i, QB)
            for p in range(PAIRS):
                lanes = slice(128 * p, 128 * p + 128)
                q2 = twice(q_s[rows, lanes])
                kk = k_s[keys, lanes]
                g2 = twice(gctx[rows, lanes])
                s = nt(q2, kk) + bias
                prob = jnp.exp(s - lse[p, blk(i, 2 * QB), :])
                dp = nt(g2, v_s[keys, lanes])
                inner = jnp.sum(prob * dp, axis=1, keepdims=True)
                ds = (prob * (dp - inner)).astype(BF)
                dq[rows, lanes] = fold(nn(ds, kk)) * 0.125
                dk[keys, lanes] += tn(ds, q2)
                dv[keys, lanes] += tn(prob.astype(BF), g2)

    def turn_back():
        @pl.loop(0, Z)
        def _(c):
            rows = blk(c, LOC)
            for p in range(PAIRS):
                lanes = slice(128 * p, 128 * p + 128)
                dqkv[rows, lanes] = rotate(dq[rows, lanes], rows, -1.0).astype(BF)
                dqkv[rows, 256 + 128 * p : 384 + 128 * p] = rotate(dk[rows, lanes], rows, -1.0).astype(BF)
            dqkv[rows, 512:] = dv[rows, :].astype(BF)
            sums = jnp.sum(dqkv[rows, :].astype(F32), axis=0, keepdims=True)
            for s in range(3):
                vsum[4 + s : 5 + s, blk(z, 256)] += sums[:, 256 * s : 256 * s + 256]

    def inward(c):
        rows = blk(c, LOC)
        g32[...] = nt(dqkv[rows, :], wqkv[...])
        h32[...] = nt(dhid[rows, :], wup[...])

        def step(i, carry):
            at = rows_at(c * LOC + i * 16, 16)
            here = blk(i, 16)
            xhat = (x_all[at, :].astype(F32) - mean_s[at, :]) * rstd_s[at, :]
            ga, gm = g32[here, :], h32[here, :]
            for k, v in enumerate((ga * xhat, gm * xhat)):
                acc[k] += v[:8] + v[8:]
            g = ga * gain_a + gm * gain_m
            if c is z:
                own_i[here, :] = g
            else:
                part_i[at, :] = g.astype(BF)
            return carry

        lax.fori_loop(0, LOC // 16, step, 0)

    def through(sums, weight):
        parts, rest = [], sums
        for _ in range(3):
            part = rest.astype(BF).astype(F32)
            parts.append(part)
            rest = rest - part
        parts.append(jnp.zeros((13, sums.shape[1]), F32))
        return jnp.sum(nt(jnp.concatenate(parts, axis=0).astype(BF), weight[...]), axis=0, keepdims=True)

    cd = FF // Z // chunks

    def weights_down():
        g_od[:, cd:, :] = tn(ctx[...], og_all[...]).reshape(chunks, cr, D).astype(BF)

        @pl.loop(0, Z)
        def _(i):
            got = tn(hidden[:, blk(i, 256)], og_all[...])
            g_od[blk(i, 256 // cd), :cd, :] = got.reshape(256 // cd, cd, D).astype(BF)

    def weights_up():
        @pl.loop(0, Z)
        def _(i):
            g_up[i] = tn(mlp_n[:, blk(i, 256)], dhid[...]).astype(BF)

    def weights_qkv():
        @pl.loop(0, Z)
        def _(c):
            g_qkv[c] = tn(attn_n[:, blk(c, 256)], dqkv[...]).astype(BF)

    class Stream:
        def __init__(self, order, grad, temp, final, across=None):
            self.order, self.idx = order, index_of(order)
            self.grad, self.temp, self.final, self.across = grad, temp, final, across
            self.v, self.g = recvs.take(bits), recvs.take(nb)
            self.zv = recvs.take(Z) if across else None
            self.first, self.size, self.off = 0, chunks, 0

        def halve(self, k):
            if k < nb:
                self.size //= 2
                b = self.order[k]
                keep = self.first + bit_of(r, b) * self.size
                give = self.first + (1 - bit_of(r, b)) * self.size
            else:
                b, keep, give = k, self.first, self.first
            self.keep = keep
            self.at = len(pending)
            go(
                self.grad(give, self.size),
                self.temp(self.off, self.size),
                sends.take(1),
                self.v + k,
                (flip(r, b), z),
            )

        def add(self, k):
            got = self.temp(self.off, self.size)
            arrived(got, self.v + k)
            keep = self.grad(self.keep, self.size)
            if k >= nb:
                pending[self.at][0].wait_send()
                pending[self.at] = None
            n = keep.shape[1] // 16

            def step(j, carry):
                i, at = lax.div(j, n), blk(lax.rem(j, n), 16)
                keep[i, at, :] = keep[i, at, :] + got[i, at, :]
                return carry

            lax.fori_loop(0, keep.shape[0] * n, step, 0, unroll=4)
            self.off += self.size
            self.first = self.keep

        def place(self):
            if self.across is None:
                self.put = local(self.grad(self.idx, 1), self.final(self.idx, 1))
                return
            src, dst = self.across
            for step in (2, 1, 3):
                t = lax.rem(z + step, Z)
                go(src(t, self.idx), dst(z, self.idx), sends.take(1), self.zv + z, (r, t))
            self.put = local(src(z, self.idx), dst(z, self.idx))

        def placed(self):
            if self.across is not None:
                for step in (1, 3, 2):
                    t = lax.rem(z + step, Z)
                    arrived(self.across[1](t, self.idx), self.zv + t)
            self.put.wait()

        def gather(self, k):
            size = 1 << k
            first = lax.div(self.idx, size) * size
            go(
                self.final(first, size),
                self.final(first, size),
                sends.take(1),
                self.g + k,
                (flip(r, self.order[nb - 1 - k]), z),
            )

        def gathered(self, k):
            size = 1 << k
            first = flip(lax.div(self.idx, size), 0) * size
            arrived(self.final(first, size), self.g + k)

    def chunk_rows(ref, lanes):
        return lambda first, n: ref.at[pl.ds(first, n), :, lanes]

    def deep_rows(ref, lanes):
        return lambda first, n: ref.at[:, pl.ds(pl.multiple_of(first * cr, cr), n * cr), lanes]

    def deep_block(ref, lanes):
        return lambda t, idx: ref.at[t, rows_at(idx * cr, cr), lanes]

    def pair(grad, temp, final, width, across):
        made = []
        for order, lanes in ((order_a, pl.ds(0, width)), (order_b, pl.ds(width, width))):
            if across:
                refs = [deep_rows(ref, lanes) for ref in (grad, temp, final)]
                both = (deep_block(grad, lanes), deep_block(final, lanes))
                made.append(Stream(order, *refs, both))
            else:
                made.append(Stream(order, *[chunk_rows(ref, lanes) for ref in (grad, temp, final)]))
        return made

    class Group:
        def __init__(self, streams):
            self.streams, self.at = streams, 0

        def all(self, name, *args):
            for s in self.streams:
                getattr(s, name)(*args)

        def go_on(self, times=1):
            for _ in range(times):
                n = self.at
                if 0 < n <= bits:
                    self.all("add", n - 1)
                if n < bits:
                    self.all("halve", n)
                elif n == bits:
                    self.all("place")
                elif n == bits + 1:
                    self.all("placed")
                else:
                    self.all("gathered", n - bits - 2)
                if bits + 1 <= n < bits + 1 + nb:
                    self.all("gather", n - bits - 1)
                self.at += 1

    down = Group(pair(g_od, t_od, f_od, 512, False))
    up = Group(pair(g_up, t_up, f_up, 512, True))
    qkv = Group(pair(g_qkv, t_qkv, f_qkv, 384, True))
    total_steps = bits + 2 + nb

    vec_steps = [(0, b) for b in range(bits)] + [(1, b) for b in range(2)]
    vec_v2 = recvs.take(len(vec_steps))
    vec_at = [0]

    def vec_on():
        n = vec_at[0]
        if n > len(vec_steps):
            return
        if n > 0:
            arrived(vrecv.at[n - 1], vec_v2 + n - 1)
            pending[vec_at[1]][0].wait_send()
            pending[vec_at[1]] = None
            vsum[...] = vsum[...] + vrecv[n - 1]
        if n < len(vec_steps):
            axis, b = vec_steps[n]
            dev = (flip(r, b), z) if axis == 0 else (r, flip(z, b))
            vec_at[1:] = [len(pending)]
            go(vsum, vrecv.at[n], sends.take(1), vec_v2 + n, dev)
        vec_at[0] += 1

    norm_rows(z)
    for j in range(1, Z):
        zz = lax.rem(z + j, Z)
        arrived(weight_region(0, zz, idx_a, 1), up_v + zz)
        for s in range(3):
            arrived(
                wqkv.at[rows_at(zz * LOC + idx_b * cr, cr), pl.ds(s * 256, 256)],
                qkv_v + zz * 3 + s,
            )
    for k in range(nb):
        weight_step(k)
        if k == 1:
            gx.hand(c1, other)
            gx.hand(c2, end)
            gg.send((0,))
        if k == nb - 1:
            gx.wait(c1)
            norm_rows(c1)
        weight_wait(k)
    own_up.wait()
    for copy in own_qkv:
        copy.wait()
    gx.hand(c3, end)
    gg.send((2,))
    project(z)
    project(c1)
    gx.wait(c2)
    norm_rows(c2)
    project(c2)
    for copy in w_own:
        copy.wait()

    @pl.when(z != 2)
    def _():
        attend(z)

    gx.wait(c3)
    gg.send((1,))
    norm_rows(c3)
    project(c3)
    gg.hand(c1, other)
    gg.hand(c2, end)
    attend(c3)
    mix(c3)
    attend(c2)
    mix(c2)
    attend(c1)
    mix(c1)
    gg.hand(c3, end)

    @pl.when(z == 2)
    def _():
        attend(z)

    mix(z)
    og_own.wait()
    side(z)
    gg.wait(c1)
    side(c1)
    attend_back(z)
    attend_back(c1)
    s_out.pass_far(middle)
    gg.wait(c2)
    side(c2)
    attend_back(c2)
    s_out.pass_other(middle)
    gg.wait(c3)
    weights_down()
    down.go_on()
    side(c3)
    weights_up()
    down.go_on()
    up.go_on()
    attend_back(c3)
    up.go_on()
    s_out.pass_end(middle)
    turn_back()
    weights_qkv()
    qkv.go_on()
    down.go_on()
    inward(c3)
    s_in.send(c3)
    qkv.go_on()
    inward(c2)
    down.go_on(2)
    up.go_on()
    inward(c1)
    s_in.send(c2)
    inward(z)
    up.go_on()
    down.go_on()
    qkv.go_on()

    def add_og(i, carry):
        return carry + og_all[rows_at(z * LOC + i * 16, 16), :].astype(F32)

    vsum[11:12, :] = jnp.sum(
        lax.fori_loop(0, LOC // 16, add_og, jnp.zeros((16, 1024), F32)), axis=0, keepdims=True
    )
    sums = jnp.concatenate([vsum[4 + s : 5 + s, blk(z, 256)] for s in range(3)], axis=1)
    vsum[0:1, :] = jnp.sum(acc[0], axis=0, keepdims=True)
    vsum[1:2, :] = through(sums, wqkv)
    vsum[2:3, :] = jnp.sum(acc[1], axis=0, keepdims=True)
    vsum[3:4, :] = through(vsum[pl.ds(7 + z, 1), :], wup)
    vec_on()
    s_in.pass_far(middle)
    s_out.finish()
    part_o[own_rows, :] = own_o[...].astype(BF)
    copies = [local(part_o.at[own_rows], outputs)]
    qkv.go_on()
    up.go_on()
    vec_on()
    s_in.send(c1)
    down.go_on()
    s_in.pass_other(middle)
    vec_on()
    up.go_on()
    qkv.go_on()
    vec_on()
    s_in.pass_end(middle)
    while qkv.at < total_steps - 1:
        qkv.go_on()
        vec_on()
        if up.at < total_steps:
            up.go_on()
        if down.at < total_steps:
            down.go_on()
    vec_on()
    s_in.finish()

    def finish(i, carry):
        rows = blk(i, 16)
        at = rows_at(z * LOC + i * 16, 16)
        rstd = rstd_s[at, :]
        xhat = (x_all[at, :].astype(F32) - mean_s[at, :]) * rstd
        g = own_i[rows, :]
        m1 = jnp.mean(g, axis=1, keepdims=True)
        m2 = jnp.mean(g * xhat, axis=1, keepdims=True)
        res = rstd * (g - m1 - xhat * m2)
        part_i[at, :] = (og_all[at, :].astype(F32) + res).astype(BF)
        return carry

    lax.fori_loop(0, LOC // 16, finish, 0, unroll=2)
    copies.append(local(part_i.at[own_rows], in_grad))
    while vec_at[0] <= len(vec_steps):
        vec_on()
    vec_out[...] = vsum[...]
    for group in (qkv, up, down):
        while group.at < total_steps:
            group.go_on()
    for copy in copies:
        copy.wait()
    for copy, when in [p for p in pending if p is not None]:
        if when is None:
            copy.wait_send()
        else:
            pl.when(when)(copy.wait_send)


def tail(outs_in, in_in, f_qkv, f_up, f_od, vec, *results):
    z = lax.axis_index("shard")
    outs, ingrad, gga, gba, ggm, gbm, gqkv, gqkvb, gout, gup, gupb, gdown, goutb = results
    outs[...] = outs_in[...]
    ingrad[...] = in_in[...]
    for t in range(Z):
        gup[:, 1024 * t : 1024 * t + 1024] = f_up[t].astype(F32)
        for s in range(3):
            first = D * s + 256 * t
            gqkv[:, first : first + 256] = f_qkv[t, :, 256 * s : 256 * s + 256].astype(F32)
    n, m = gdown.shape[0] // f_od.shape[0], gout.shape[0] // f_od.shape[0]
    for i in range(f_od.shape[0]):
        gdown[n * i : n * i + n, :] = f_od[i, :n].astype(F32)
        gout[m * i : m * i + m, :] = f_od[i, n:].astype(F32)

    @pl.when(pl.program_id(0) == 0)
    def _():
        for k, ref in ((0, gga), (1, gba), (2, ggm), (3, gbm), (11, goutb)):
            ref[...] = vec[k : k + 1, blk(z, 256)].reshape(256)
        for i in range(3):
            g = 3 * z + i
            piece = vec[pl.ds(4 + lax.div(g, Z), 1), blk(lax.rem(g, Z), 256)]
            gqkvb[256 * i : 256 * i + 256] = piece.reshape(256)
        gupb[...] = vec[pl.ds(7 + z, 1), :].reshape(1024)


def shards(
    replicas,
    inputs,
    out_grad,
    segment_ids,
    ln_gain_attn,
    ln_bias_attn,
    ln_gain_mlp,
    ln_bias_mlp,
    qkv_weight,
    qkv_bias,
    out_weight,
    up_weight,
    up_bias,
    down_weight,
    output_bias,
):
    bits = int(math.log2(replicas))
    chunks = 1 << min(bits, 4)
    vm = pl.BlockSpec(memory_space=pltpu.VMEM)
    hbm = pl.BlockSpec(memory_space=pl.ANY)

    def v(*shape, dtype=BF):
        return pltpu.VMEM(shape, dtype)

    scratch = dict(
        x_all=v(TOK, D),
        og_all=v(TOK, D),
        gain_a_all=v(D),
        bias_a_all=v(D),
        gain_m_all=v(D),
        bias_m_all=v(D),
        bias_o_all=v(D),
        qkv_b_all=v(3 * D),
        up_b=v(1024),
        seg=pltpu.VMEM((1, TOK), jnp.int32),
        tab_c=v(TOK, 128, dtype=F32),
        tab_a=v(TOK, 128, dtype=F32),
        tab_b=v(TOK, 128, dtype=F32),
        start=v(TOK, 1, dtype=F32),
        wqkv=v(D, 768),
        wup=v(D, 1024),
        wout=v(256, D),
        wdown=v(1024, D),
        attn_n=v(TOK, D),
        mlp_n=v(TOK, D),
        mean_s=v(TOK, 1, dtype=F32),
        rstd_s=v(TOK, 1, dtype=F32),
        q_s=v(TOK, 256),
        k_s=v(TOK, 256),
        v_s=v(TOK, 256),
        ctx=v(TOK, 256),
        lse=v(PAIRS, 2 * TOK, 1, dtype=F32),
        h32=v(LOC, 1024, dtype=F32),
        g32=v(LOC, 1024, dtype=F32),
        acc=v(2, 8, 1024, dtype=F32),
        hidden=v(TOK, 1024),
        dgelu=v(TOK, 1024),
        part_o=v(TOK, D),
        part_i=v(TOK, D),
        own_o=v(LOC, D, dtype=F32),
        own_i=v(LOC, D, dtype=F32),
        land_o=v(5 * LOC, D),
        land_i=v(5 * LOC, D),
        gctx=v(TOK, 256),
        dq=v(TOK, 256, dtype=F32),
        dk=v(TOK, 256, dtype=F32),
        dv=v(TOK, 256, dtype=F32),
        dqkv=v(TOK, 768),
        g_qkv=v(Z, 256, 768),
        g_up=v(Z, 256, 1024),
        g_od=v(chunks, 1280 // chunks, D),
        t_qkv=v(Z, 256, 768),
        t_up=v(Z, 256, 1024),
        t_od=v(chunks, 1280 // chunks, D),
        vsum=v(16, 1024, dtype=F32),
        vrecv=v(bits + 2, 16, 1024, dtype=F32),
        ssem=pltpu.SemaphoreType.DMA((NSEM,)),
        rsem=pltpu.SemaphoreType.DMA((NSEM,)),
        lsem=pltpu.SemaphoreType.DMA((32,)),
    )
    names = list(scratch)

    def body(*refs):
        layer(replicas, *refs[:20], **dict(zip(names, refs[20:])))

    res = pl.pallas_call(
        body,
        out_shape=[
            jax.ShapeDtypeStruct((LOC, D), BF),
            jax.ShapeDtypeStruct((LOC, D), BF),
            jax.ShapeDtypeStruct((Z, 256, 768), BF),
            jax.ShapeDtypeStruct((Z, 256, 1024), BF),
            jax.ShapeDtypeStruct((chunks, 1280 // chunks, D), BF),
            jax.ShapeDtypeStruct((16, 1024), F32),
        ],
        in_specs=[hbm] * 14,
        out_specs=[hbm, hbm, hbm, hbm, hbm, vm],
        scratch_shapes=list(scratch.values()),
        compiler_params=pltpu.CompilerParams(
            collective_id=0,
            has_side_effects=True,
            vmem_limit_bytes=61 * 2**20,
        ),
    )(
        inputs.reshape(LOC, D),
        out_grad.reshape(LOC, D),
        qkv_weight,
        up_weight,
        out_weight,
        down_weight,
        ln_gain_attn,
        ln_bias_attn,
        ln_gain_mlp,
        ln_bias_mlp,
        output_bias,
        qkv_bias,
        up_bias,
        segment_ids,
    )
    steps = chunks // 2
    n = LOC // steps
    row = pl.BlockSpec((n, D), lambda i: (i, 0))
    tall = pl.BlockSpec((1024 // steps, D), lambda i: (i, 0))

    def fixed(w):
        return pl.BlockSpec((w,), lambda i: (0,))

    small, wide = [fixed(256)], [fixed(768)]
    final = pl.pallas_call(
        tail,
        grid=(steps,),
        in_specs=[
            row,
            row,
            pl.BlockSpec((Z, n, 768), lambda i: (0, i, 0)),
            pl.BlockSpec((Z, n, 1024), lambda i: (0, i, 0)),
            pl.BlockSpec((2, 1280 // chunks, D), lambda i: (i, 0, 0)),
            pl.BlockSpec((16, 1024), lambda i: (0, 0)),
        ],
        out_specs=[row, row]
        + small * 4
        + [pl.BlockSpec((n, 3 * D), lambda i: (i, 0))]
        + wide
        + [row, pl.BlockSpec((n, FF), lambda i: (i, 0)), fixed(1024), tall]
        + small,
        out_shape=[jax.ShapeDtypeStruct((LOC, D), BF)] * 2
        + [jax.ShapeDtypeStruct((256,), F32)] * 4
        + [
            jax.ShapeDtypeStruct((256, 3 * D), F32),
            jax.ShapeDtypeStruct((768,), F32),
            jax.ShapeDtypeStruct((256, D), F32),
            jax.ShapeDtypeStruct((256, FF), F32),
            jax.ShapeDtypeStruct((1024,), F32),
            jax.ShapeDtypeStruct((1024, D), F32),
            jax.ShapeDtypeStruct((256,), F32),
        ],
    )(*res)
    return tuple(a.reshape(1, LOC, D) for a in final[:2]) + tuple(final[2:])


def solution(mesh):
    seq = P("replica", "shard", None)
    row = P("shard", None)
    one = P("shard")
    return jax.shard_map(
        partial(shards, mesh.shape["replica"]),
        mesh=mesh,
        in_specs=(seq, seq, P("replica", None), one, one, one, one, row, one, row, row, one, row, one),
        out_specs=(seq, seq, one, one, one, one, row, one, row, row, one, row, one),
        check_vma=False,
    )
```

```python
import math
from functools import partial

import jax
import jax.numpy as jnp
import numpy as np
from jax import lax
from jax.experimental import pallas as pl
from jax.experimental.pallas import tpu as pltpu
from jax.sharding import PartitionSpec as P

D = 1024
FF = 4096
HEADS = 16
HEAD = 64
ROT = 16
Z = 4
LOC = 256
TOK = 1024
PAIRS = 2
QB = 128
KB = 640
EPS = 1e-05
BF = jnp.bfloat16
F32 = jnp.float32
MESH = pl.DeviceIdType.MESH
NSEM = 256
SUB = 2


def bit_of(value, place):
    return lax.rem(lax.div(value, 1 << place), 2)


def flip(value, place):
    return value + (1 - 2 * bit_of(value, place)) * (1 << place)


def nn(a, b):
    return jnp.dot(a, b, preferred_element_type=F32)


def nt(a, b):
    return lax.dot_general(a, b, (((1,), (1,)), ((), ())), preferred_element_type=F32)


def tn(a, b):
    return lax.dot_general(a, b, (((0,), (0,)), ((), ())), preferred_element_type=F32)


def blk(i, n):
    return pl.ds(pl.multiple_of(i * n, n), n)


class Count:
    def __init__(self):
        self.used = 0

    def take(self, n):
        first = self.used
        self.used += n
        assert self.used <= NSEM
        return first


def layer(
    replicas,
    x_in,
    og_in,
    qkv_w,
    up_w,
    out_w,
    down_w,
    gain_a_in,
    bias_a_in,
    gain_m_in,
    bias_m_in,
    bias_o_in,
    qkv_b_in,
    up_b_in,
    seg_in,
    outputs,
    in_grad,
    f_qkv,
    f_up,
    f_od,
    vec_out,
    x_all,
    og_all,
    gain_a_all,
    bias_a_all,
    gain_m_all,
    bias_m_all,
    bias_o_all,
    qkv_b_all,
    up_b,
    seg,
    tab_c,
    tab_a,
    tab_b,
    start,
    wqkv,
    wup,
    wout,
    wdown,
    attn_n,
    mlp_n,
    mean_s,
    rstd_s,
    q_s,
    k_s,
    v_s,
    ctx,
    lse,
    h32,
    g32,
    acc,
    hidden,
    dgelu,
    part_o,
    part_i,
    own_o,
    own_i,
    land_o,
    land_i,
    gctx,
    dq,
    dk,
    dv,
    dqkv,
    g_qkv,
    g_up,
    g_od,
    t_qkv,
    t_up,
    t_od,
    vsum,
    vrecv,
    ssem,
    rsem,
    lsem,
):
    r = lax.axis_index("replica")
    z = lax.axis_index("shard")
    bits = int(math.log2(replicas))
    nb = min(bits, 4)
    chunks = 1 << nb
    sends, recvs, locals_ = Count(), Count(), Count()
    pending = []

    middle = (z == 1) | (z == 2)
    ends = (z == 0) | (z == 3)
    low = z < 2
    end = jnp.where(low, 0, 3)
    mid = jnp.where(low, 1, 2)
    other = 3 - mid
    far = 3 - end
    beside = z + 1 - 2 * lax.rem(z, 2)
    c1, c2, c3 = beside, other, far
    own_rows = blk(z, LOC)

    def remote(src, dst, s, v, dev):
        return pltpu.make_async_remote_copy(
            src_ref=src,
            dst_ref=dst,
            send_sem=ssem.at[s],
            recv_sem=rsem.at[v],
            device_id=dev,
            device_id_type=MESH,
        )

    def go(src, dst, s, v, dev, when=None):
        copy = remote(src, dst, s, v, dev)
        if when is None:
            copy.start()
        else:
            pl.when(when)(copy.start)
        pending.append((copy, when))

    def arrived(dst, v, when=None):
        copy = remote(dst, dst, 0, v, (r, z))
        if when is None:
            copy.wait_recv()
        else:
            pl.when(when)(copy.wait_recv)

    def local(src, dst):
        copy = pltpu.make_async_copy(src, dst, lsem.at[locals_.take(1)])
        copy.start()
        return copy

    def rows_at(first, n):
        return pl.ds(pl.multiple_of(first, n), n)

    small = [
        (gain_a_in, gain_a_all),
        (bias_a_in, bias_a_all),
        (gain_m_in, gain_m_all),
        (bias_m_in, bias_m_all),
        (bias_o_in, bias_o_all),
        (qkv_b_in, qkv_b_all),
    ]

    def share(ref, src, c):
        return ref.at[blk(c, src.shape[0])]

    vec_own = [local(src, share(dst, src, z)) for src, dst in small] + [local(up_b_in, up_b)]
    seg_own = local(seg_in, seg)
    x_own = local(x_in, x_all.at[own_rows])

    barrier = pltpu.get_barrier_semaphore()
    for step in range(1, Z):
        pl.semaphore_signal(
            barrier, inc=1, device_id=(r, lax.rem(z + step, Z)), device_id_type=MESH
        )
    for b in range(bits):
        pl.semaphore_signal(barrier, inc=1, device_id=(flip(r, b), z), device_id_type=MESH)
    pl.semaphore_wait(barrier, Z - 1 + bits)

    order_a = list(range(nb))
    order_b = [0, *reversed(range(1, nb))]

    def index_of(order):
        return sum(bit_of(r, b) * (1 << (nb - 1 - k)) for k, b in enumerate(order))

    idx_a, idx_b = index_of(order_a), index_of(order_b)
    cr = LOC // chunks

    up_v, qkv_v, vec_v = recvs.take(Z), recvs.take(3 * Z), recvs.take(6 * Z)
    for step in (1, 3, 2):
        t = lax.rem(z + step, Z)
        for i, (src, dst) in enumerate(small):
            go(src, share(dst, src, z), sends.take(1), vec_v + i * Z + z, (r, t))
    for step in (1, 3, 2):
        t = lax.rem(z + step, Z)
        go(
            up_w.at[blk(idx_a, cr), blk(t, 1024)],
            wup.at[rows_at(z * LOC + idx_a * cr, cr)],
            sends.take(1),
            up_v + z,
            (r, t),
        )
        for s in range(3):
            go(
                qkv_w.at[blk(idx_b, cr), rows_at(s * D + t * 256, 256)],
                wqkv.at[rows_at(z * LOC + idx_b * cr, cr), pl.ds(s * 256, 256)],
                sends.take(1),
                qkv_v + z * 3 + s,
                (r, t),
            )

    piece = LOC // SUB

    class Gather:
        def __init__(self, src, buf):
            self.src, self.buf = src, buf
            self.v = recvs.take(Z * SUB)

        def rows(self, c, k):
            return self.buf.at[rows_at(c * LOC + k * piece, piece)]

        def send(self, ways=(0, 1, 2)):
            every = ((mid, ends), (end, middle), (other, middle))
            for k in range(SUB):
                for dev, when in [every[w] for w in ways]:
                    go(
                        self.src.at[pl.ds(k * piece, piece)],
                        self.rows(z, k),
                        sends.take(1),
                        self.v + z * SUB + k,
                        (r, dev),
                        when,
                    )

        def hand(self, c, dev):
            for k in range(SUB):
                arrived(self.rows(c, k), self.v + c * SUB + k, middle)
                go(
                    self.rows(c, k),
                    self.rows(c, k),
                    sends.take(1),
                    self.v + c * SUB + k,
                    (r, dev),
                    middle,
                )

        def wait(self, c):
            for k in range(SUB):
                arrived(self.rows(c, k), self.v + c * SUB + k, ends)

    gx, gg = Gather(x_in, x_all), Gather(og_in, og_all)
    gx.send()
    own_up = local(up_w.at[:, blk(z, 1024)], wup.at[own_rows])
    own_qkv = [
        local(qkv_w.at[:, rows_at(s * D + z * 256, 256)], wqkv.at[own_rows, pl.ds(s * 256, 256)])
        for s in range(3)
    ]
    og_own = local(og_in, og_all.at[own_rows])
    w_own = [local(out_w, wout), local(down_w, wdown)]

    ag_v = recvs.take(3 * 2 * nb)

    def weight_region(kind, zz, first, n):
        ref = wup if kind == 0 else wqkv
        return ref.at[pl.ds(pl.multiple_of(zz * LOC + first * cr, cr), n * cr)]

    def weight_step(k):
        for j in range(1, Z):
            zz = lax.rem(z + j, Z)
            for kind, order, idx in ((0, order_a, idx_a), (1, order_b, idx_b)):
                b = order[nb - 1 - k]
                size = 1 << k
                first = lax.div(idx, size) * size
                go(
                    weight_region(kind, zz, first, size),
                    weight_region(kind, zz, first, size),
                    sends.take(1),
                    ag_v + ((j - 1) * 2 + kind) * nb + k,
                    (flip(r, b), z),
                )

    def weight_wait(k):
        for j in range(1, Z):
            zz = lax.rem(z + j, Z)
            for kind, idx in ((0, idx_a), (1, idx_b)):
                size = 1 << k
                first = flip(lax.div(idx, size), 0) * size
                arrived(weight_region(kind, zz, first, size), ag_v + ((j - 1) * 2 + kind) * nb + k)

    seg_own.wait()
    lane = lax.broadcasted_iota(jnp.int32, (QB, 128), 1)
    turned = lax.rem(lane, HEAD) < ROT
    ids = seg[...]
    count0 = jnp.sum((ids == 0).astype(F32), axis=1, keepdims=True)
    count1 = jnp.sum((ids <= 1).astype(F32), axis=1, keepdims=True)
    begin = jnp.where(ids == 0, 0.0, jnp.where(ids == 1, count0, count1))
    begin8 = jnp.broadcast_to(begin, (8, TOK))
    position = lax.broadcasted_iota(jnp.int32, (8, TOK), 1).astype(F32) - begin8
    turn = lax.broadcasted_iota(jnp.int32, (8, TOK), 0)
    freq = jnp.zeros((8, TOK), F32)
    for i in range(ROT // 2):
        rate = np.float32(1.0) / np.float32(10000.0) ** np.float32(i * 2.0 / ROT)
        freq = jnp.where(turn == i, float(rate), freq)
    angles = position * freq
    cosines, sines = jnp.cos(angles), jnp.sin(angles)
    for i in range(TOK // 128):
        at = slice(128 * i, 128 * i + 128)
        cosine, sine, first = cosines[:, at], sines[:, at], begin8[:, at]
        none = jnp.zeros_like(cosine)
        half = [cosine, cosine, -sine, none, none, sine, first, none]
        wide = jnp.concatenate(half + half, axis=0).T
        tab_c[at, :] = jnp.where(turned, wide, 1.0)
        tab_a[at, :] = jnp.where(turned, pltpu.roll(wide, 112, 1), 0.0)
        tab_b[at, :] = jnp.where(turned, pltpu.roll(wide, 96, 1), 0.0)
        start[at, :] = wide[:, 48:49]

    for copy in vec_own:
        copy.wait()
    x_own.wait()
    for j in range(1, Z):
        zz = lax.rem(z + j, Z)
        for i, (src, dst) in enumerate(small):
            arrived(share(dst, src, zz), vec_v + i * Z + zz)

    def flat(piece):
        return piece.astype(F32).reshape(1, piece.shape[0])

    gain_a, bias_a, gain_m, bias_m, bias_o = [flat(dst[...]) for _, dst in small[:5]]
    qkv_b = [flat(qkv_b_all[blk(s * Z + z, 256)]) for s in range(3)]
    up_shift = flat(up_b[...])

    def norm_rows(c):
        def norm(i, carry):
            rows = rows_at(c * LOC + i * 16, 16)
            v = x_all[rows, :].astype(F32)
            mean = jnp.mean(v, axis=1, keepdims=True)
            cen = v - mean
            rstd = lax.rsqrt(jnp.mean(cen * cen, axis=1, keepdims=True) + EPS)
            xhat = cen * rstd
            attn_n[rows, :] = (xhat * gain_a + bias_a).astype(BF)
            mlp_n[rows, :] = (xhat * gain_m + bias_m).astype(BF)
            mean_s[rows, :] = mean
            rstd_s[rows, :] = rstd
            return carry

        lax.fori_loop(0, LOC // 16, norm, 0, unroll=2)

    def rotate(t, rows, sign):
        return (
            t * tab_c[rows, :]
            + sign * (pltpu.roll(t, 120, 1) * tab_a[rows, :])
            + sign * (pltpu.roll(t, 8, 1) * tab_b[rows, :])
        )

    def project(c):
        rows = blk(c, LOC)
        res = nn(attn_n[rows, :], wqkv[...])
        for p in range(PAIRS):
            lanes = slice(128 * p, 128 * p + 128)
            t = res[:, lanes] + qkv_b[0][:, lanes]
            q_s[rows, lanes] = (rotate(t, rows, 1.0) * 0.125).astype(BF)
            t = res[:, 256 + 128 * p : 384 + 128 * p] + qkv_b[1][:, lanes]
            k_s[rows, lanes] = rotate(t, rows, 1.0).astype(BF)
        v_s[rows, :] = (res[:, 512:] + qkv_b[2]).astype(BF)
        h32[...] = nn(mlp_n[rows, :], wup[...])

        def act(i, carry):
            v = h32[blk(i, 16), :] + up_shift
            cdf = 0.5 + 0.5 * lax.erf(v * (0.5**0.5))
            at = rows_at(c * LOC + i * 16, 16)
            hidden[at, :] = (v * cdf).astype(BF)
            dgelu[at, :] = (
                cdf + v * jnp.exp(-0.5 * v * v) * (1.0 / math.sqrt(2.0 * math.pi))
            ).astype(BF)
            return carry

        lax.fori_loop(0, LOC // 16, act, 0)

    def twice(t):
        zero = jnp.zeros_like(t)
        return jnp.concatenate(
            [jnp.where(lane < HEAD, t, zero), jnp.where(lane >= HEAD, t, zero)], axis=0
        )

    def fold(t):
        return jnp.where(lane < HEAD, t[:QB], t[QB:])

    def window(i):
        first = pl.multiple_of(jnp.maximum(i * QB - (KB - QB), 0), QB)
        at = first + lax.broadcasted_iota(jnp.int32, (QB, KB), 1)
        row = i * QB + lax.broadcasted_iota(jnp.int32, (QB, KB), 0)
        ok = (at <= row) & (at.astype(F32) >= start[blk(i, QB), :])
        bias = jnp.where(ok, 0.0, -1e30)
        return pl.ds(first, KB), jnp.concatenate([bias, bias], axis=0)

    def attend(c):
        @pl.loop(0, LOC // QB)
        def _(j):
            i = c * (LOC // QB) + j
            keys, bias = window(i)
            rows = blk(i, QB)
            for p in range(PAIRS):
                lanes = slice(128 * p, 128 * p + 128)
                s = nt(twice(q_s[rows, lanes]), k_s[keys, lanes]) + bias
                top = jnp.max(s, axis=1, keepdims=True)
                e = jnp.exp(s - top)
                total = jnp.sum(e, axis=1, keepdims=True)
                lse[p, blk(i, 2 * QB), :] = top + jnp.log(total)
                prob = (e * (1.0 / total)).astype(BF)
                ctx[rows, lanes] = fold(nn(prob, v_s[keys, lanes])).astype(BF)

    class Scatter:
        def __init__(self, part, own, land):
            self.part, self.own, self.land = part, own, land
            self.v = recvs.take(5 * SUB)

        def slot(self, s, k):
            return self.land.at[rows_at(s * LOC + k * piece, piece)]

        def rows(self, c, k):
            return self.part.at[rows_at(c * LOC + k * piece, piece)]

        def send(self, c):
            place = jnp.clip(jnp.where(low, 3 - c, c), 0, 2)
            when = ends & (c != z)
            for k in range(SUB):
                go(
                    self.rows(c, k),
                    self.slot(place, k),
                    sends.take(1),
                    self.v + place * SUB + k,
                    (r, mid),
                    when,
                )

        def pass_on(self, came, c, dev, goes, when):
            for k in range(SUB):
                arrived(self.slot(came, k), self.v + came * SUB + k, when)

                @pl.when(when)
                def _():
                    def add(i, carry):
                        at = rows_at(c * LOC + k * piece + i * 16, 16)
                        got = rows_at(came * LOC + k * piece + i * 16, 16)
                        self.part[at, :] = self.part[at, :] + self.land[got, :]
                        return carry

                    lax.fori_loop(0, piece // 16, add, 0, unroll=2)

                go(
                    self.rows(c, k),
                    self.slot(goes, k),
                    sends.take(1),
                    self.v + goes * SUB + k,
                    (r, dev),
                    when,
                )

        def pass_far(self, when):
            self.pass_on(0, far, other, 3, when)

        def pass_other(self, when):
            self.pass_on(1, other, other, 4, when)

        def pass_end(self, when):
            self.pass_on(3, end, end, 0, when)

        def finish(self):
            for came, when in ((0, ends), (2, middle), (4, middle)):
                for k in range(SUB):
                    arrived(self.slot(came, k), self.v + came * SUB + k, when)

                @pl.when(when)
                def _():
                    def add(i, carry):
                        got = self.land[rows_at(came * LOC + i * 16, 16), :]
                        self.own[blk(i, 16), :] += got.astype(F32)
                        return carry

                    lax.fori_loop(0, LOC // 16, add, 0, unroll=2)

    s_out = Scatter(part_o, own_o, land_o)
    s_in = Scatter(part_i, own_i, land_i)

    def mix(c):
        rows = blk(c, LOC)
        res = nn(ctx[rows, :], wout[...]) + nn(hidden[rows, :], wdown[...])
        if c is z:
            own_o[...] = res + x_all[own_rows, :].astype(F32) + bias_o
        else:
            part_o[rows, :] = res.astype(BF)
            s_out.send(c)

    vsum[...] = jnp.zeros_like(vsum)
    acc[...] = jnp.zeros_like(acc)
    dk[...] = jnp.zeros_like(dk)
    dv[...] = jnp.zeros_like(dv)

    def side(c):
        rows = blk(c, LOC)
        gctx[rows, :] = nt(og_all[rows, :], wout[...]).astype(BF)
        h32[...] = nt(og_all[rows, :], wdown[...])

        def act(i, carry):
            at = rows_at(c * LOC + i * 16, 16)
            g = (h32[blk(i, 16), :] * dgelu[at, :].astype(F32)).astype(BF)
            dgelu[at, :] = g
            return carry + g.astype(F32)

        total = lax.fori_loop(0, LOC // 16, act, jnp.zeros((16, 1024), F32), unroll=2)
        vsum[pl.ds(7 + z, 1), :] += jnp.sum(total, axis=0, keepdims=True)

    dhid = dgelu

    def attend_back(c):
        @pl.loop(0, LOC // QB)
        def _(j):
            i = c * (LOC // QB) + j
            keys, bias = window(i)
            rows = blk(i, QB)
            for p in range(PAIRS):
                lanes = slice(128 * p, 128 * p + 128)
                q2 = twice(q_s[rows, lanes])
                kk = k_s[keys, lanes]
                g2 = twice(gctx[rows, lanes])
                s = nt(q2, kk) + bias
                prob = jnp.exp(s - lse[p, blk(i, 2 * QB), :])
                dp = nt(g2, v_s[keys, lanes])
                inner = jnp.sum(prob * dp, axis=1, keepdims=True)
                ds = (prob * (dp - inner)).astype(BF)
                dq[rows, lanes] = fold(nn(ds, kk)) * 0.125
                dk[keys, lanes] += tn(ds, q2)
                dv[keys, lanes] += tn(prob.astype(BF), g2)

    def turn_back():
        @pl.loop(0, Z)
        def _(c):
            rows = blk(c, LOC)
            for p in range(PAIRS):
                lanes = slice(128 * p, 128 * p + 128)
                dqkv[rows, lanes] = rotate(dq[rows, lanes], rows, -1.0).astype(BF)
                dqkv[rows, 256 + 128 * p : 384 + 128 * p] = rotate(dk[rows, lanes], rows, -1.0).astype(BF)
            dqkv[rows, 512:] = dv[rows, :].astype(BF)
            sums = jnp.sum(dqkv[rows, :].astype(F32), axis=0, keepdims=True)
            for s in range(3):
                vsum[4 + s : 5 + s, blk(z, 256)] += sums[:, 256 * s : 256 * s + 256]

    def inward(c):
        rows = blk(c, LOC)
        g32[...] = nt(dqkv[rows, :], wqkv[...])
        h32[...] = nt(dhid[rows, :], wup[...])

        def step(i, carry):
            at = rows_at(c * LOC + i * 16, 16)
            here = blk(i, 16)
            xhat = (x_all[at, :].astype(F32) - mean_s[at, :]) * rstd_s[at, :]
            ga, gm = g32[here, :], h32[here, :]
            for k, v in enumerate((ga * xhat, gm * xhat)):
                acc[k] += v[:8] + v[8:]
            g = ga * gain_a + gm * gain_m
            if c is z:
                own_i[here, :] = g
            else:
                part_i[at, :] = g.astype(BF)
            return carry

        lax.fori_loop(0, LOC // 16, step, 0, unroll=2)

    def through(sums, weight):
        parts, rest = [], sums
        for _ in range(3):
            part = rest.astype(BF).astype(F32)
            parts.append(part)
            rest = rest - part
        parts.append(jnp.zeros((13, sums.shape[1]), F32))
        return jnp.sum(nt(jnp.concatenate(parts, axis=0).astype(BF), weight[...]), axis=0, keepdims=True)

    cd = FF // Z // chunks

    def weights_down():
        g_od[:, cd:, :] = tn(ctx[...], og_all[...]).reshape(chunks, cr, D).astype(BF)

        @pl.loop(0, Z)
        def _(i):
            got = tn(hidden[:, blk(i, 256)], og_all[...])
            g_od[blk(i, 256 // cd), :cd, :] = got.reshape(256 // cd, cd, D).astype(BF)

    def weights_up():
        @pl.loop(0, Z)
        def _(i):
            g_up[i] = tn(mlp_n[:, blk(i, 256)], dhid[...]).astype(BF)

    def weights_qkv():
        @pl.loop(0, Z)
        def _(c):
            g_qkv[c] = tn(attn_n[:, blk(c, 256)], dqkv[...]).astype(BF)

    class Stream:
        def __init__(self, order, grad, temp, final, across=None):
            self.order, self.idx = order, index_of(order)
            self.grad, self.temp, self.final, self.across = grad, temp, final, across
            self.v, self.g = recvs.take(bits), recvs.take(nb)
            self.zv = recvs.take(Z) if across else None
            self.first, self.size, self.off = 0, chunks, 0

        def halve(self, k):
            if k < nb:
                self.size //= 2
                b = self.order[k]
                keep = self.first + bit_of(r, b) * self.size
                give = self.first + (1 - bit_of(r, b)) * self.size
            else:
                b, keep, give = k, self.first, self.first
            self.keep = keep
            self.at = len(pending)
            go(
                self.grad(give, self.size),
                self.temp(self.off, self.size),
                sends.take(1),
                self.v + k,
                (flip(r, b), z),
            )

        def add(self, k):
            got = self.temp(self.off, self.size)
            arrived(got, self.v + k)
            keep = self.grad(self.keep, self.size)
            if k >= nb:
                pending[self.at][0].wait_send()
                pending[self.at] = None
            n = keep.shape[1] // 16

            def step(j, carry):
                i, at = lax.div(j, n), blk(lax.rem(j, n), 16)
                keep[i, at, :] = keep[i, at, :] + got[i, at, :]
                return carry

            lax.fori_loop(0, keep.shape[0] * n, step, 0, unroll=4)
            self.off += self.size
            self.first = self.keep

        def place(self):
            if self.across is None:
                self.put = local(self.grad(self.idx, 1), self.final(self.idx, 1))
                return
            src, dst = self.across
            for step in (2, 1, 3):
                t = lax.rem(z + step, Z)
                go(src(t, self.idx), dst(z, self.idx), sends.take(1), self.zv + z, (r, t))
            self.put = local(src(z, self.idx), dst(z, self.idx))

        def placed(self):
            if self.across is not None:
                for step in (1, 3, 2):
                    t = lax.rem(z + step, Z)
                    arrived(self.across[1](t, self.idx), self.zv + t)
            self.put.wait()

        def gather(self, k):
            size = 1 << k
            first = lax.div(self.idx, size) * size
            go(
                self.final(first, size),
                self.final(first, size),
                sends.take(1),
                self.g + k,
                (flip(r, self.order[nb - 1 - k]), z),
            )

        def gathered(self, k):
            size = 1 << k
            first = flip(lax.div(self.idx, size), 0) * size
            arrived(self.final(first, size), self.g + k)

    def chunk_rows(ref, lanes):
        return lambda first, n: ref.at[pl.ds(first, n), :, lanes]

    def deep_rows(ref, lanes):
        return lambda first, n: ref.at[:, pl.ds(pl.multiple_of(first * cr, cr), n * cr), lanes]

    def deep_block(ref, lanes):
        return lambda t, idx: ref.at[t, rows_at(idx * cr, cr), lanes]

    def pair(grad, temp, final, width, across):
        made = []
        for order, lanes in ((order_a, pl.ds(0, width)), (order_b, pl.ds(width, width))):
            if across:
                refs = [deep_rows(ref, lanes) for ref in (grad, temp, final)]
                both = (deep_block(grad, lanes), deep_block(final, lanes))
                made.append(Stream(order, *refs, both))
            else:
                made.append(Stream(order, *[chunk_rows(ref, lanes) for ref in (grad, temp, final)]))
        return made

    class Group:
        def __init__(self, streams):
            self.streams, self.at = streams, 0

        def all(self, name, *args):
            for s in self.streams:
                getattr(s, name)(*args)

        def go_on(self, times=1):
            for _ in range(times):
                n = self.at
                if 0 < n <= bits:
                    self.all("add", n - 1)
                if n < bits:
                    self.all("halve", n)
                elif n == bits:
                    self.all("place")
                elif n == bits + 1:
                    self.all("placed")
                else:
                    self.all("gathered", n - bits - 2)
                if bits + 1 <= n < bits + 1 + nb:
                    self.all("gather", n - bits - 1)
                self.at += 1

    down = Group(pair(g_od, t_od, f_od, 512, False))
    up = Group(pair(g_up, t_up, f_up, 512, True))
    qkv = Group(pair(g_qkv, t_qkv, f_qkv, 384, True))
    total_steps = bits + 2 + nb

    vec_steps = [(0, b) for b in range(bits)] + [(1, b) for b in range(2)]
    vec_v2 = recvs.take(len(vec_steps))
    vec_at = [0]

    def vec_on():
        n = vec_at[0]
        if n > len(vec_steps):
            return
        if n > 0:
            arrived(vrecv.at[n - 1], vec_v2 + n - 1)
            pending[vec_at[1]][0].wait_send()
            pending[vec_at[1]] = None
            vsum[...] = vsum[...] + vrecv[n - 1]
        if n < len(vec_steps):
            axis, b = vec_steps[n]
            dev = (flip(r, b), z) if axis == 0 else (r, flip(z, b))
            vec_at[1:] = [len(pending)]
            go(vsum, vrecv.at[n], sends.take(1), vec_v2 + n, dev)
        vec_at[0] += 1

    norm_rows(z)
    for j in range(1, Z):
        zz = lax.rem(z + j, Z)
        arrived(weight_region(0, zz, idx_a, 1), up_v + zz)
        for s in range(3):
            arrived(
                wqkv.at[rows_at(zz * LOC + idx_b * cr, cr), pl.ds(s * 256, 256)],
                qkv_v + zz * 3 + s,
            )
    for k in range(nb):
        weight_step(k)
        if k == 1:
            gx.hand(c1, other)
            gx.hand(c2, end)
            gg.send((0,))
        if k == nb - 1:
            gx.wait(c1)
            norm_rows(c1)
        weight_wait(k)
    own_up.wait()
    for copy in own_qkv:
        copy.wait()
    gx.hand(c3, end)
    gg.send((2,))
    project(z)
    project(c1)
    gx.wait(c2)
    norm_rows(c2)
    project(c2)
    for copy in w_own:
        copy.wait()

    @pl.when(z != 2)
    def _():
        attend(z)

    gx.wait(c3)
    gg.send((1,))
    norm_rows(c3)
    project(c3)
    gg.hand(c1, other)
    gg.hand(c2, end)
    attend(c3)
    mix(c3)
    attend(c2)
    mix(c2)
    attend(c1)
    mix(c1)
    gg.hand(c3, end)

    @pl.when(z == 2)
    def _():
        attend(z)

    mix(z)
    og_own.wait()
    side(z)
    gg.wait(c1)
    side(c1)
    attend_back(z)
    attend_back(c1)
    s_out.pass_far(middle)
    gg.wait(c2)
    side(c2)
    attend_back(c2)
    s_out.pass_other(middle)
    gg.wait(c3)
    weights_down()
    down.go_on()
    side(c3)
    weights_up()
    down.go_on()
    up.go_on()
    attend_back(c3)
    up.go_on()
    s_out.pass_end(middle)
    turn_back()
    weights_qkv()
    qkv.go_on()
    down.go_on()
    inward(c3)
    s_in.send(c3)
    qkv.go_on()
    inward(c2)
    down.go_on(2)
    up.go_on()
    inward(c1)
    s_in.send(c2)
    inward(z)
    up.go_on()
    down.go_on()
    qkv.go_on()

    def add_og(i, carry):
        return carry + og_all[rows_at(z * LOC + i * 16, 16), :].astype(F32)

    vsum[11:12, :] = jnp.sum(
        lax.fori_loop(0, LOC // 16, add_og, jnp.zeros((16, 1024), F32)), axis=0, keepdims=True
    )
    sums = jnp.concatenate([vsum[4 + s : 5 + s, blk(z, 256)] for s in range(3)], axis=1)
    vsum[0:1, :] = jnp.sum(acc[0], axis=0, keepdims=True)
    vsum[1:2, :] = through(sums, wqkv)
    vsum[2:3, :] = jnp.sum(acc[1], axis=0, keepdims=True)
    vsum[3:4, :] = through(vsum[pl.ds(7 + z, 1), :], wup)
    vec_on()
    s_in.pass_far(middle)
    s_out.finish()
    part_o[own_rows, :] = own_o[...].astype(BF)
    copies = [local(part_o.at[own_rows], outputs)]
    qkv.go_on()
    up.go_on()
    vec_on()
    s_in.send(c1)
    down.go_on()
    s_in.pass_other(middle)
    vec_on()
    up.go_on()
    qkv.go_on()
    vec_on()
    s_in.pass_end(middle)
    while qkv.at < total_steps - 1:
        qkv.go_on()
        vec_on()
        if up.at < total_steps:
            up.go_on()
        if down.at < total_steps:
            down.go_on()
    vec_on()
    s_in.finish()

    def finish(i, carry):
        rows = blk(i, 16)
        at = rows_at(z * LOC + i * 16, 16)
        rstd = rstd_s[at, :]
        xhat = (x_all[at, :].astype(F32) - mean_s[at, :]) * rstd
        g = own_i[rows, :]
        m1 = jnp.mean(g, axis=1, keepdims=True)
        m2 = jnp.mean(g * xhat, axis=1, keepdims=True)
        res = rstd * (g - m1 - xhat * m2)
        part_i[at, :] = (og_all[at, :].astype(F32) + res).astype(BF)
        return carry

    lax.fori_loop(0, LOC // 16, finish, 0, unroll=2)
    copies.append(local(part_i.at[own_rows], in_grad))
    while vec_at[0] <= len(vec_steps):
        vec_on()
    vec_out[...] = vsum[...]
    for group in (qkv, up, down):
        while group.at < total_steps:
            group.go_on()
    for copy in copies:
        copy.wait()
    for copy, when in [p for p in pending if p is not None]:
        if when is None:
            copy.wait_send()
        else:
            pl.when(when)(copy.wait_send)


def tail(outs_in, in_in, f_qkv, f_up, f_od, vec, *results):
    z = lax.axis_index("shard")
    outs, ingrad, gga, gba, ggm, gbm, gqkv, gqkvb, gout, gup, gupb, gdown, goutb = results
    outs[...] = outs_in[...]
    ingrad[...] = in_in[...]
    for t in range(Z):
        gup[:, 1024 * t : 1024 * t + 1024] = f_up[t].astype(F32)
        for s in range(3):
            first = D * s + 256 * t
            gqkv[:, first : first + 256] = f_qkv[t, :, 256 * s : 256 * s + 256].astype(F32)
    n, m = gdown.shape[0] // f_od.shape[0], gout.shape[0] // f_od.shape[0]
    for i in range(f_od.shape[0]):
        gdown[n * i : n * i + n, :] = f_od[i, :n].astype(F32)
        gout[m * i : m * i + m, :] = f_od[i, n:].astype(F32)

    @pl.when(pl.program_id(0) == 0)
    def _():
        for k, ref in ((0, gga), (1, gba), (2, ggm), (3, gbm), (11, goutb)):
            ref[...] = vec[k : k + 1, blk(z, 256)].reshape(256)
        for i in range(3):
            g = 3 * z + i
            piece = vec[pl.ds(4 + lax.div(g, Z), 1), blk(lax.rem(g, Z), 256)]
            gqkvb[256 * i : 256 * i + 256] = piece.reshape(256)
        gupb[...] = vec[pl.ds(7 + z, 1), :].reshape(1024)


def shards(
    replicas,
    inputs,
    out_grad,
    segment_ids,
    ln_gain_attn,
    ln_bias_attn,
    ln_gain_mlp,
    ln_bias_mlp,
    qkv_weight,
    qkv_bias,
    out_weight,
    up_weight,
    up_bias,
    down_weight,
    output_bias,
):
    bits = int(math.log2(replicas))
    chunks = 1 << min(bits, 4)
    vm = pl.BlockSpec(memory_space=pltpu.VMEM)
    hbm = pl.BlockSpec(memory_space=pl.ANY)

    def v(*shape, dtype=BF):
        return pltpu.VMEM(shape, dtype)

    scratch = dict(
        x_all=v(TOK, D),
        og_all=v(TOK, D),
        gain_a_all=v(D),
        bias_a_all=v(D),
        gain_m_all=v(D),
        bias_m_all=v(D),
        bias_o_all=v(D),
        qkv_b_all=v(3 * D),
        up_b=v(1024),
        seg=pltpu.VMEM((1, TOK), jnp.int32),
        tab_c=v(TOK, 128, dtype=F32),
        tab_a=v(TOK, 128, dtype=F32),
        tab_b=v(TOK, 128, dtype=F32),
        start=v(TOK, 1, dtype=F32),
        wqkv=v(D, 768),
        wup=v(D, 1024),
        wout=v(256, D),
        wdown=v(1024, D),
        attn_n=v(TOK, D),
        mlp_n=v(TOK, D),
        mean_s=v(TOK, 1, dtype=F32),
        rstd_s=v(TOK, 1, dtype=F32),
        q_s=v(TOK, 256),
        k_s=v(TOK, 256),
        v_s=v(TOK, 256),
        ctx=v(TOK, 256),
        lse=v(PAIRS, 2 * TOK, 1, dtype=F32),
        h32=v(LOC, 1024, dtype=F32),
        g32=v(LOC, 1024, dtype=F32),
        acc=v(2, 8, 1024, dtype=F32),
        hidden=v(TOK, 1024),
        dgelu=v(TOK, 1024),
        part_o=v(TOK, D),
        part_i=v(TOK, D),
        own_o=v(LOC, D, dtype=F32),
        own_i=v(LOC, D, dtype=F32),
        land_o=v(5 * LOC, D),
        land_i=v(5 * LOC, D),
        gctx=v(TOK, 256),
        dq=v(TOK, 256, dtype=F32),
        dk=v(TOK, 256, dtype=F32),
        dv=v(TOK, 256, dtype=F32),
        dqkv=v(TOK, 768),
        g_qkv=v(Z, 256, 768),
        g_up=v(Z, 256, 1024),
        g_od=v(chunks, 1280 // chunks, D),
        t_qkv=v(Z, 256, 768),
        t_up=v(Z, 256, 1024),
        t_od=v(chunks, 1280 // chunks, D),
        vsum=v(16, 1024, dtype=F32),
        vrecv=v(bits + 2, 16, 1024, dtype=F32),
        ssem=pltpu.SemaphoreType.DMA((NSEM,)),
        rsem=pltpu.SemaphoreType.DMA((NSEM,)),
        lsem=pltpu.SemaphoreType.DMA((32,)),
    )
    names = list(scratch)

    def body(*refs):
        layer(replicas, *refs[:20], **dict(zip(names, refs[20:])))

    res = pl.pallas_call(
        body,
        out_shape=[
            jax.ShapeDtypeStruct((LOC, D), BF),
            jax.ShapeDtypeStruct((LOC, D), BF),
            jax.ShapeDtypeStruct((Z, 256, 768), BF),
            jax.ShapeDtypeStruct((Z, 256, 1024), BF),
            jax.ShapeDtypeStruct((chunks, 1280 // chunks, D), BF),
            jax.ShapeDtypeStruct((16, 1024), F32),
        ],
        in_specs=[hbm] * 14,
        out_specs=[hbm, hbm, hbm, hbm, hbm, vm],
        scratch_shapes=list(scratch.values()),
        compiler_params=pltpu.CompilerParams(
            collective_id=0,
            has_side_effects=True,
            vmem_limit_bytes=61 * 2**20,
        ),
    )(
        inputs.reshape(LOC, D),
        out_grad.reshape(LOC, D),
        qkv_weight,
        up_weight,
        out_weight,
        down_weight,
        ln_gain_attn,
        ln_bias_attn,
        ln_gain_mlp,
        ln_bias_mlp,
        output_bias,
        qkv_bias,
        up_bias,
        segment_ids,
    )
    steps = chunks // 2
    n = LOC // steps
    row = pl.BlockSpec((n, D), lambda i: (i, 0))
    tall = pl.BlockSpec((1024 // steps, D), lambda i: (i, 0))

    def fixed(w):
        return pl.BlockSpec((w,), lambda i: (0,))

    small, wide = [fixed(256)], [fixed(768)]
    final = pl.pallas_call(
        tail,
        grid=(steps,),
        in_specs=[
            row,
            row,
            pl.BlockSpec((Z, n, 768), lambda i: (0, i, 0)),
            pl.BlockSpec((Z, n, 1024), lambda i: (0, i, 0)),
            pl.BlockSpec((2, 1280 // chunks, D), lambda i: (i, 0, 0)),
            pl.BlockSpec((16, 1024), lambda i: (0, 0)),
        ],
        out_specs=[row, row]
        + small * 4
        + [pl.BlockSpec((n, 3 * D), lambda i: (i, 0))]
        + wide
        + [row, pl.BlockSpec((n, FF), lambda i: (i, 0)), fixed(1024), tall]
        + small,
        out_shape=[jax.ShapeDtypeStruct((LOC, D), BF)] * 2
        + [jax.ShapeDtypeStruct((256,), F32)] * 4
        + [
            jax.ShapeDtypeStruct((256, 3 * D), F32),
            jax.ShapeDtypeStruct((768,), F32),
            jax.ShapeDtypeStruct((256, D), F32),
            jax.ShapeDtypeStruct((256, FF), F32),
            jax.ShapeDtypeStruct((1024,), F32),
            jax.ShapeDtypeStruct((1024, D), F32),
            jax.ShapeDtypeStruct((256,), F32),
        ],
    )(*res)
    return tuple(a.reshape(1, LOC, D) for a in final[:2]) + tuple(final[2:])


def solution(mesh):
    seq = P("replica", "shard", None)
    row = P("shard", None)
    one = P("shard")
    return jax.shard_map(
        partial(shards, mesh.shape["replica"]),
        mesh=mesh,
        in_specs=(seq, seq, P("replica", None), one, one, one, one, row, one, row, row, one, row, one),
        out_specs=(seq, seq, one, one, one, one, row, one, row, row, one, row, one),
        check_vma=False,
    )
```
